128 devices in a mesh: seq: 64 (over x, z, y), head: 2 (over core).
Axes of the slice: x: 4, y: 4, z: 4, core: 2. Of those that a mesh axis runs over, the one named last changes fastest.
Arguments:
- video_query: bfloat16 [32768, 3072], P('seq', 'head'), as said below
- video_value: bfloat16 [32768, 3072], P('seq', 'head'), may hold values from -12 to 12
- audio_key: bfloat16 [16384, 3072], P('seq', 'head'), as said below
- audio_value: bfloat16 [16384, 3072], P('seq', 'head'), may hold values from -12 to 12
- video_proj: bfloat16 [3072, 3072], P('head'), may hold values from -0.109375 to 0.109375
- audio_proj: bfloat16 [3072, 3072], P('head'), may hold values from -0.109375 to 0.109375
- pair_first: int32 [64], replicated, may hold values from 0 to 63, as said below
- pair_count: int32 [64], replicated, may hold values from 1 to 5, as said below
Outputs:
- video_out: bfloat16 [32768, 3072], P('seq', 'head')
- audio_out: bfloat16 [16384, 3072], P('seq', 'head')
The draws below stay inside these ranges and needn't reach their ends.
Inputs may be any that keep to these rules, and one draw needn't show every extreme that they name: Video block b pairs with the audio blocks pair_first[b] to pair_first[b] + pair_count[b] - 1; these lie within b - 2 to b + 2, inside 0 to 63, and always include block b. `pair_count`: some video block pairs with 5 audio blocks in every draw. `video_query`: entries lie within -8 to 8. `audio_key`: entries lie within -8 to 8.
All inputs are finite; a program needn't handle non-finite values.
Results may differ from the reference program's by a relative error of at most 0.0052.
Values may be sent and summed in bfloat16 or wider, within the bound.
No kernel may reach another device: no remote copies, remote signals or barrier semaphores. Data moves between devices by JAX's collectives and lax.ppermute only.
A program may use at most 192 MiB of HBM per device.

```python
import math
import jax
import jax.numpy as jnp
from jax import lax

D = 3072
HEADS = 24
HEAD_DIM = 128
VID_DEV = 512
AUD_DEV = 256
HALF = 2
NB = 64
C = 3072
VTOK = 32768
ATOK = 16384
N_SEQ = 64


def pair_window(key):
    window_key = jax.random.fold_in(key, 21)
    left = jax.random.randint(window_key, (NB,), 0, HALF + 1)
    right = jax.random.randint(jax.random.fold_in(window_key, 1), (NB,), 0, HALF + 1)
    blocks = jnp.arange(NB, dtype=jnp.int32)
    middle = blocks == NB // 2
    left = jnp.where(middle, HALF, left)
    right = jnp.where(middle, HALF, right)
    left = jnp.where(blocks == NB - 1, 0, left)
    right = jnp.where(blocks == 0, 0, right)
    first = jnp.maximum(blocks - left, 0)
    last = jnp.minimum(blocks + right, NB - 1)
    return (first.astype(jnp.int32), (last - first + 1).astype(jnp.int32))


def draw_video_query(key, part):
    key = jax.random.fold_in(key, 1)
    base = 1.5 * jax.random.normal(key, (VTOK, HEADS * HEAD_DIM), jnp.float32)
    return jnp.clip(base, -8.0, 8.0).astype(jnp.bfloat16)


def draw_audio_key(key, part):
    key = jax.random.fold_in(key, 2)
    base = 1.5 * jax.random.normal(key, (ATOK, HEADS * HEAD_DIM), jnp.float32)
    return jnp.clip(base, -8.0, 8.0).astype(jnp.bfloat16)


def draw_pair_first(key, part):
    first, count = pair_window(key)
    return first


def draw_pair_count(key, part):
    first, count = pair_window(key)
    return count


def levels(rng, dims, split, low, largest):
    loudness, own = 1.0, jax.random.fold_in(rng, 6)
    for position, parts in split:
        steps = jnp.exp(jax.random.uniform(jax.random.fold_in(own, position), (parts,), jnp.float32, low / len(split), largest / len(split)))
        loudness = loudness * jnp.repeat(steps, dims[position] // parts).reshape([-1 if axis == position else 1 for axis in range(len(dims))])
    return loudness


def normal_values(stream_key, extent, deviation, limit, cuts=(), held_as=jnp.bfloat16):
    entries = deviation * jax.random.normal(stream_key, extent, jnp.float32)
    if cuts:
        entries = entries * levels(stream_key, extent, cuts, -0.22, 0.18)
    return jnp.clip(entries, -limit, limit).astype(held_as)


def setup_inputs(seed: int = 0) -> dict:
    key_of = jax.random.split(jax.random.key(seed), 9)
    return {
        "video_query": draw_video_query(jax.random.fold_in(key_of[8], 71), 0),
        "video_value": normal_values(key_of[1], (VTOK, C), 2.0, 12.0, ((0, 64), (1, 2))),
        "audio_key": draw_audio_key(jax.random.fold_in(key_of[8], 71), 0),
        "audio_value": normal_values(key_of[3], (ATOK, C), 2.0, 12.0, ((0, 64), (1, 2))),
        "video_proj": normal_values(key_of[4], (C, D), C ** -0.5, 0.109375, ((0, 2),)),
        "audio_proj": normal_values(key_of[5], (C, D), C ** -0.5, 0.109375, ((0, 2),)),
        "pair_first": draw_pair_first(jax.random.fold_in(key_of[8], 71), 0),
        "pair_count": draw_pair_count(jax.random.fold_in(key_of[8], 71), 0),
    }


NEG = -1e+30

def tile_scores(query, keys):
    return jnp.einsum('vhe,ahe->hva', query.astype(jnp.float32), keys.astype(jnp.float32)) / math.sqrt(HEAD_DIM)

def row_piece(scores, values):
    top = lax.optimization_barrier(jnp.max(scores, axis=2))
    expo = jnp.exp(scores - top[:, :, None])
    total = lax.optimization_barrier(jnp.sum(expo, axis=2))
    weights = expo.astype(jnp.bfloat16)
    out = jnp.einsum('hva,ahe->vhe', weights.astype(jnp.float32), values.astype(jnp.float32))
    return (top, total, out)

def col_piece(scores, values):
    top = lax.optimization_barrier(jnp.max(scores, axis=1))
    expo = jnp.exp(scores - top[:, None, :])
    total = lax.optimization_barrier(jnp.sum(expo, axis=1))
    weights = expo.astype(jnp.bfloat16)
    out = jnp.einsum('hva,vhe->ahe', weights.astype(jnp.float32), values.astype(jnp.float32))
    return (top, total, out)

def masked(part, valid):
    top, total, out = part
    return (jnp.where(valid, top, NEG), jnp.where(valid, total, 0.0), jnp.where(valid, out, 0.0))

def combine(acc, part):
    top_a, total_a, out_a = acc
    top_b, total_b, out_b = part
    top = jnp.maximum(top_a, top_b)
    old = jnp.exp(top_a - top)
    new = jnp.exp(top_b - top)
    return (top, total_a * old + total_b * new, out_a * old.T[:, :, None] + out_b * new.T[:, :, None])

def empty_acc(rows):
    return (jnp.full((HEADS, rows), NEG, jnp.float32), jnp.zeros((HEADS, rows), jnp.float32), jnp.zeros((rows, HEADS, HEAD_DIM), jnp.float32))

def finish(acc):
    top, total, out = acc
    return (out / total.T[:, :, None]).astype(jnp.bfloat16)

def reference(video_query, video_value, audio_key, audio_value, video_proj, audio_proj, pair_first, pair_count):
    nblocks = N_SEQ
    vid_query = video_query.reshape(nblocks, VID_DEV, HEADS, HEAD_DIM)
    vid_value = video_value.reshape(nblocks, VID_DEV, HEADS, HEAD_DIM)
    aud_key = audio_key.reshape(nblocks, AUD_DEV, HEADS, HEAD_DIM)
    aud_value = audio_value.reshape(nblocks, AUD_DEV, HEADS, HEAD_DIM)

    def video_block(index):
        first = pair_first[index]
        count = pair_count[index]
        query = vid_query[index]
        acc = empty_acc(VID_DEV)
        for step in range(2 * HALF + 1):
            target = jnp.minimum(first + step, nblocks - 1).astype(jnp.int32)
            part = row_piece(tile_scores(query, aud_key[target]), aud_value[target])
            acc = combine(acc, masked(part, step < count))
        return finish(acc)

    def audio_block(index):
        keys = aud_key[index]
        acc = empty_acc(AUD_DEV)
        for offset in range(-HALF, HALF + 1):
            source = index + offset
            clipped = jnp.clip(source, 0, nblocks - 1).astype(jnp.int32)
            valid = (source >= 0) & (source < nblocks) & (pair_first[clipped] <= index) & (index < pair_first[clipped] + pair_count[clipped])
            part = col_piece(tile_scores(vid_query[clipped], keys), vid_value[clipped])
            acc = combine(acc, masked(part, valid))
        return finish(acc)
    blocks = jnp.arange(nblocks, dtype=jnp.int32)
    video_attn = lax.map(video_block, blocks).reshape(nblocks * VID_DEV, HEADS * HEAD_DIM)
    audio_attn = lax.map(audio_block, blocks).reshape(nblocks * AUD_DEV, HEADS * HEAD_DIM)
    video_out = jnp.dot(video_attn, video_proj, preferred_element_type=jnp.float32).astype(jnp.bfloat16)
    audio_out = jnp.dot(audio_attn, audio_proj, preferred_element_type=jnp.float32).astype(jnp.bfloat16)
    return (video_out, audio_out)
```

```python
import functools
import math

import jax
import jax.numpy as jnp
from jax import lax
from jax.experimental import pallas as pl
from jax.experimental.pallas import tpu as pltpu
from jax.sharding import PartitionSpec as P

HD = 128
LINE = 4
GH = 3
GW = GH * HD
VID = 512
AUD = 256
NEG = -1e30
SCALE = math.log2(math.e) / math.sqrt(HD)
EXTRA = 16
BF = jnp.bfloat16
F32 = jnp.float32
ANY = pl.BlockSpec(memory_space=pl.ANY)
SMEM = pl.BlockSpec(memory_space=pltpu.SMEM)
VMEM = pl.BlockSpec(memory_space=pltpu.VMEM)


def group_cols(g):
    return pl.ds(pl.multiple_of(g * GW, HD), GW)


def run_copies(copies):
    for copy in copies:
        copy.start()
    for copy in copies:
        copy.wait()


def pack_kernel(me, a, b, out1, out2, out3, sem):
    y = lax.rem(me[0], LINE)
    copies = []
    for d, out in ((1, out1), (3, out3), (2, out2)):
        cols = group_cols(lax.rem(y + d, LINE))
        copies.append(pltpu.make_async_copy(a.at[:, cols], out.at[0], sem.at[2 * d]))
        copies.append(pltpu.make_async_copy(b.at[:, cols], out.at[1], sem.at[2 * d + 1]))
    run_copies(copies)


def pack(me, a, b):
    piece = jax.ShapeDtypeStruct((2, a.shape[0], GW), BF)
    return pl.pallas_call(
        pack_kernel,
        out_shape=(piece,) * 3,
        in_specs=[SMEM, ANY, ANY],
        out_specs=(ANY,) * 3,
        scratch_shapes=[pltpu.SemaphoreType.DMA((8,))],
        name="pack",
    )(me, a, b)


def line_kernel(me, k, v, kv1, kv2, kv3, low, high, sem):
    y = lax.rem(me[0], LINE)
    cols = group_cols(y)
    for d, got in ((0, None), (1, kv1), (2, kv2), (3, kv3)):
        j = lax.rem(y + LINE - d, LINE)

        def place(out, at):
            if d == 0:
                pltpu.make_async_copy(k.at[:, cols], out.at[at, 0], sem.at[0]).start()
                pltpu.make_async_copy(v.at[:, cols], out.at[at, 1], sem.at[4]).start()
            else:
                pltpu.make_async_copy(got, out.at[at], sem.at[d]).start()

        @pl.when(j < 2)
        def _():
            place(low, j)

        @pl.when(j >= 2)
        def _():
            place(high, j - 2)

    pltpu.make_async_copy(k.at[:, cols], low.at[0, 0], sem.at[0]).wait()
    pltpu.make_async_copy(v.at[:, cols], low.at[0, 1], sem.at[4]).wait()
    for d, got in ((1, kv1), (2, kv2), (3, kv3)):
        pltpu.make_async_copy(got, low.at[0], sem.at[d]).wait()


def line_blocks(me, k, v, kv1, kv2, kv3):
    half = jax.ShapeDtypeStruct((2, 2, AUD, GW), BF)
    return pl.pallas_call(
        line_kernel,
        out_shape=(half, half),
        in_specs=[SMEM] + [ANY] * 5,
        out_specs=(ANY, ANY),
        scratch_shapes=[pltpu.SemaphoreType.DMA((5,))],
        name="line_blocks",
    )(me, k, v, kv1, kv2, kv3)


def attend_kernel(steps, own, carried, last, *refs):
    refs = list(refs)

    def take(n):
        part = refs[:n]
        del refs[:n]
        return part

    me, first, count = take(3)
    kvs = take(4)
    q_own, v_own = take(2) if own else (None, None)
    arrived = take(len(steps) - (1 if own else 0))
    u_in, c_in = take(2) if carried else (None, None)
    outs = take(len(steps))
    if last:
        before, after, u_out, c_out = take(4)
    else:
        u_out, c_out = take(2)
    kbuf, qbuf, obuf, tbuf, mbuf, cbuf, abuf, vtbuf, ubuf, csum, sem = refs

    y = lax.rem(me[0], LINE)
    base = me[0] - y
    copies = []

    def copy(src, dst):
        copies.append(pltpu.make_async_copy(src, dst, sem.at[len(copies)]))

    for i, part in enumerate(kvs):
        copy(part, kbuf.at[pl.ds(2 * i, 2)])
    if own:
        copy(q_own.at[:, group_cols(y)], qbuf.at[0, 0])
        copy(v_own.at[:, group_cols(y)], qbuf.at[0, 1])
    for i, part in enumerate(arrived):
        copy(part, qbuf.at[i + (1 if own else 0)])
    if carried:
        copy(u_in, ubuf)
        copy(c_in, csum)
    for c in copies:
        c.start()
    if not carried:
        ubuf[...] = jnp.zeros_like(ubuf)
        csum[...] = jnp.full_like(csum, NEG)
    for c in copies:
        c.wait()

    def video(i, carry):
        step = jnp.int32(steps[0])
        for n in range(1, len(steps)):
            step = jnp.where(i == n, steps[n], step)
        v = lax.rem(y + LINE - step, LINE)
        lo = first[base + v] - base + 2
        hi = lo + count[base + v]
        mbuf[...] = jnp.full_like(mbuf, NEG)

        def scores(a, carry):
            slot = a - lo
            for h in range(GH):
                cols = slice(h * HD, (h + 1) * HD)
                t = lax.dot_general(
                    qbuf[i, 0, :, cols], kbuf[a, 0, :, cols], (((1,), (1,)), ((), ())), preferred_element_type=F32
                )
                t = t * SCALE
                tbuf[h, slot] = t
                mbuf[h] = jnp.maximum(mbuf[h], jnp.maximum(t[:, :HD], t[:, HD:]))
                cbuf[h, slot] = jnp.broadcast_to(jnp.max(t, axis=0, keepdims=True), (8, AUD))
            return carry

        lax.fori_loop(lo, hi, scores, 0)
        for h in range(GH):
            cols = slice(h * HD, (h + 1) * HD)
            mbuf[h] = jnp.broadcast_to(jnp.max(mbuf[h], axis=1, keepdims=True), (VID, HD))
            abuf[h] = jnp.zeros((VID, 2 * HD), F32)
            vtbuf[h, :HD] = qbuf[i, 1, :, cols].T
            vtbuf[h, HD:] = jnp.ones((EXTRA, VID), BF)

        def weights(a, carry):
            slot = a - lo
            for h in range(GH):
                cols = slice(h * HD, (h + 1) * HD)
                t = tbuf[h, slot]
                r = mbuf[h]
                c = cbuf[h, slot, 0:1]
                by_row = jnp.exp2(t - jnp.concatenate([r, r], axis=1)).astype(BF)
                values = jnp.concatenate([kbuf[a, 1, :, cols], jnp.ones((AUD, HD), BF)], axis=1)
                abuf[h] += jnp.dot(by_row, values, preferred_element_type=F32)
                by_col = jnp.exp2(t - c).astype(BF)
                u = jnp.dot(vtbuf[h], by_col, preferred_element_type=F32)
                old = csum[h, a, 0:1]
                new = jnp.maximum(old, c)
                ubuf[h, a] = ubuf[h, a] * jnp.exp2(old - new) + u * jnp.exp2(c - new)
                csum[h, a] = jnp.broadcast_to(new, (8, AUD))
            return carry

        lax.fori_loop(lo, hi, weights, 0)
        for h in range(GH):
            obuf[i, :, h * HD : (h + 1) * HD] = (abuf[h, :, :HD] / abuf[h, :, HD:]).astype(BF)
        return carry

    lax.fori_loop(0, len(steps), video, 0)

    copies = [pltpu.make_async_copy(obuf.at[i], out, sem.at[i]) for i, out in enumerate(outs)]
    for c in copies:
        c.start()
    if last:
        row = lax.broadcasted_iota(jnp.int32, (EXTRA, AUD), 0)
        for place, out in ((0, before), (6, after)):
            for j in range(2):
                for h in range(GH):
                    u = ubuf[h, place + j, :HD]
                    n = ubuf[h, place + j, HD : HD + 1]
                    some = n > 0.0
                    safe = jnp.where(some, n, 1.0)
                    out[j, h, :HD] = (u / safe).astype(BF)
                    level = jnp.where(some, csum[h, place + j, 0:1] + jnp.log2(safe), NEG)
                    hi = level.astype(BF).astype(F32)
                    mid = (level - hi).astype(BF).astype(F32)
                    lo = level - hi - mid
                    parts = jnp.where(row == 0, hi, jnp.where(row == 1, mid, jnp.where(row == 2, lo, 0.0)))
                    out[j, h, HD:] = parts.astype(BF)
        for h in range(GH):
            u_out[h] = ubuf[h, 2:6]
            c_out[h] = csum[h, 2:6]
    else:
        more = [
            pltpu.make_async_copy(ubuf, u_out, sem.at[len(outs)]),
            pltpu.make_async_copy(csum, c_out, sem.at[len(outs) + 1]),
        ]
        for c in more:
            c.start()
        copies += more
    for c in copies:
        c.wait()


def attend(steps, info, kvs, own, arrived, sums, last):
    n = len(steps)
    n_idx = 2 * LINE
    out_shape = [jax.ShapeDtypeStruct((VID, GW), BF)] * n
    out_specs = [ANY] * n
    if last:
        halo = jax.ShapeDtypeStruct((2, GH, HD + EXTRA, AUD), BF)
        out_shape += [halo, halo]
        out_shape += [
            jax.ShapeDtypeStruct((GH, LINE, HD + EXTRA, AUD), F32),
            jax.ShapeDtypeStruct((GH, LINE, 8, AUD), F32),
        ]
        out_specs += [VMEM] * 4
    else:
        out_shape += [
            jax.ShapeDtypeStruct((GH, n_idx, HD + EXTRA, AUD), F32),
            jax.ShapeDtypeStruct((GH, n_idx, 8, AUD), F32),
        ]
        out_specs += [ANY] * 2
    operands = [*info, *kvs, *own, *arrived, *sums]
    tiles = 4 * n * GH
    return pl.pallas_call(
        functools.partial(attend_kernel, steps, bool(own), bool(sums), last),
        out_shape=tuple(out_shape),
        in_specs=[SMEM] * 3 + [ANY] * (len(operands) - 3),
        out_specs=tuple(out_specs),
        scratch_shapes=[
            pltpu.VMEM((n_idx, 2, AUD, GW), BF),
            pltpu.VMEM((n, 2, VID, GW), BF),
            pltpu.VMEM((n, VID, GW), BF),
            pltpu.VMEM((GH, 5, VID, AUD), F32),
            pltpu.VMEM((GH, VID, HD), F32),
            pltpu.VMEM((GH, 5, 8, AUD), F32),
            pltpu.VMEM((GH, VID, 2 * HD), F32),
            pltpu.VMEM((GH, HD + EXTRA, VID), BF),
            pltpu.VMEM((GH, n_idx, HD + EXTRA, AUD), F32),
            pltpu.VMEM((GH, n_idx, 8, AUD), F32),
            pltpu.SemaphoreType.DMA((12,)),
        ],
        compiler_params=pltpu.CompilerParams(vmem_limit_bytes=40 * 2**20),
        cost_estimate=pl.CostEstimate(
            flops=tiles * 6 * VID * AUD * HD, bytes_accessed=8 * 2**20, transcendentals=tiles * 2 * VID * AUD
        ),
        name="attend_last" if last else "attend",
    )(*operands)


def merge_kernel(me, u, c, prev, nxt, out0, out1, out2, out3):
    y = lax.rem(me[0], LINE)
    for d, out in enumerate((out0, out1, out2, out3)):
        j = lax.rem(y + d, LINE)
        for h in range(GH):
            low = j < 2
            at = lax.rem(j, 2)
            got = jnp.where(low, prev[at, h].astype(F32), nxt[at, h].astype(F32))
            level = got[HD : HD + 1] + got[HD + 1 : HD + 2] + got[HD + 2 : HD + 3]
            n = u[h, j, HD : HD + 1]
            own = c[h, j, 0:1] + jnp.log2(n)
            top = jnp.maximum(own, level)
            own_w = jnp.exp2(own - top)
            got_w = jnp.exp2(level - top)
            total = own_w + got_w
            mixed = u[h, j, :HD] * (own_w / (n * total)) + got[:HD] * (got_w / total)
            out[:, h * HD : (h + 1) * HD] = mixed.T.astype(BF)


def merge(me, u, c, prev, nxt):
    return pl.pallas_call(
        merge_kernel,
        out_shape=(jax.ShapeDtypeStruct((AUD, GW), BF),) * LINE,
        in_specs=[SMEM] + [VMEM] * 4,
        out_specs=(VMEM,) * LINE,
        name="merge",
        compiler_params=pltpu.CompilerParams(vmem_limit_bytes=24 * 2**20),
    )(me, u, c, prev, nxt)


def project_kernel(place, *refs):
    mine, theirs = refs[:LINE], refs[LINE : 2 * LINE]
    w_mine, w_theirs, out, left, right = refs[2 * LINE :]
    y = place[0]

    @pl.when(pl.program_id(0) == 0)
    def _():
        for d in range(LINE):
            cols = group_cols(lax.rem(y + d, LINE))
            left[:, cols] = mine[d][...]
            right[:, cols] = theirs[d][...]

    total = jnp.dot(left[...], w_mine[...], preferred_element_type=F32)
    total += jnp.dot(right[...], w_theirs[...], preferred_element_type=F32)
    out[...] = total.astype(BF)


def project(place, mine, theirs, w, w_theirs):
    rows = mine[0].shape[0]
    width = w_theirs.shape[1]
    tile = 256
    full = pl.BlockSpec((rows, GW), lambda n, s: (0, 0))
    return pl.pallas_call(
        project_kernel,
        out_shape=jax.ShapeDtypeStruct((rows, width), BF),
        grid_spec=pltpu.PrefetchScalarGridSpec(
            num_scalar_prefetch=1,
            grid=(width // tile,),
            in_specs=[full] * (2 * LINE)
            + [
                pl.BlockSpec((w.shape[0], tile), lambda n, s: (0, s[1] * (width // tile) + n)),
                pl.BlockSpec((w.shape[0], tile), lambda n, s: (0, n)),
            ],
            out_specs=pl.BlockSpec((rows, tile), lambda n, s: (0, n)),
            scratch_shapes=[pltpu.VMEM((rows, LINE * GW), BF), pltpu.VMEM((rows, LINE * GW), BF)],
        ),
        compiler_params=pltpu.CompilerParams(vmem_limit_bytes=32 * 2**20),
        cost_estimate=pl.CostEstimate(
            flops=4 * rows * w.shape[0] * width, bytes_accessed=4 * w.shape[0] * width, transcendentals=0
        ),
        name="project",
    )(place, *mine, *theirs, w, w_theirs)


def shards(
    video_query, video_value, audio_key, audio_value, video_proj, audio_proj, pair_first, pair_count
):
    nblocks = lax.axis_size("seq")
    me = lax.axis_index("seq").astype(jnp.int32)
    core = lax.axis_index("head").astype(jnp.int32)
    me_arr = me[None]
    place = jnp.stack([lax.rem(me, LINE), core])

    def along_line(x, d):
        return lax.ppermute(
            x, "seq", [(s, s // LINE * LINE + (s + d) % LINE) for s in range(nblocks)]
        )

    def across_lines(x, d):
        return lax.ppermute(x, "seq", [(s, (s + d * LINE) % nblocks) for s in range(nblocks)])

    def swap(x):
        return lax.ppermute(x, "head", [(0, 1), (1, 0)])

    kv_out = pack(me_arr, audio_key, audio_value)
    kv = [along_line(kv_out[d - 1], d) for d in (1, 2, 3)]
    qv_out = pack(me_arr, video_query, video_value)
    qv = [along_line(qv_out[d - 1], d) for d in (1, 2, 3)]
    low, high = line_blocks(me_arr, audio_key, audio_value, *kv)
    before, after = across_lines(high, 1), across_lines(low, -1)

    width = video_proj.shape[1] // 2
    v_other = swap(lax.dynamic_slice_in_dim(video_proj, (1 - core) * width, width, 1))
    a_other = swap(lax.dynamic_slice_in_dim(audio_proj, (1 - core) * width, width, 1))

    info = (me_arr, pair_first, pair_count)
    kvs = (before, low, high, after)
    o0, o1, o3, u, c = attend(
        (0, 1, 3), info, kvs, (video_query, video_value), (qv[0], qv[2]), (), False
    )
    o2, to_prev, to_next, u, c = attend((2,), info, kvs, (), (qv[1],), (u, c), True)
    from_next, from_prev = across_lines(to_prev, -1), across_lines(to_next, 1)

    v1, v3, v2 = along_line(o1, -1), along_line(o3, -3), along_line(o2, -2)
    v_mine = (o0, v1, v2, v3)
    near = swap(jnp.stack([o0, v1, v3]))
    far = swap(v2)
    v_theirs = (near[0], near[1], far, near[2])
    video_out = project(place, v_mine, v_theirs, video_proj, v_other)

    m0, m1, m2, m3 = merge(me_arr, u, c, from_prev, from_next)
    a_mine = (m0, along_line(m3, 3), along_line(m2, 2), along_line(m1, 1))
    a_all = swap(jnp.stack(a_mine))
    audio_out = project(place, a_mine, tuple(a_all[d] for d in range(LINE)), audio_proj, a_other)
    return video_out, audio_out


def solution(mesh):
    in_specs = (
        P("seq", "head"),
        P("seq", "head"),
        P("seq", "head"),
        P("seq", "head"),
        P("head", None),
        P("head", None),
        P(),
        P(),
    )
    out_specs = (P("seq", "head"), P("seq", "head"))
    return jax.shard_map(shards, mesh=mesh, in_specs=in_specs, out_specs=out_specs, check_vma=False)
```

```python
import functools
import math

import jax
import jax.numpy as jnp
from jax import lax
from jax.experimental import pallas as pl
from jax.experimental.pallas import tpu as pltpu
from jax.sharding import PartitionSpec as P

HD = 128
LINE = 4
GH = 3
GW = GH * HD
VID = 512
AUD = 256
NEG = -1e30
SCALE = math.log2(math.e) / math.sqrt(HD)
EXTRA = 16
BF = jnp.bfloat16
F32 = jnp.float32
MIB = 2**20


def cost(us):
    return pl.CostEstimate(flops=int(us * 1e9), bytes_accessed=1000, transcendentals=0)


TINY = cost(0.001)
ANY = pl.BlockSpec(memory_space=pl.ANY)
SMEM = pl.BlockSpec(memory_space=pltpu.SMEM)
VMEM = pl.BlockSpec(memory_space=pltpu.VMEM)


def group_cols(g):
    return pl.ds(pl.multiple_of(g * GW, HD), GW)


def through(pieces, held, sem):
    ins = [pltpu.make_async_copy(src, held.at[at], sem.at[0, i]) for i, (src, at, _) in enumerate(pieces)]
    outs = [pltpu.make_async_copy(held.at[at], dst, sem.at[1, i]) for i, (_, at, dst) in enumerate(pieces)]
    for copy in ins:
        copy.start()
    for copy, out in zip(ins, outs):
        copy.wait()
        out.start()
    for copy in outs:
        copy.wait()


def pack_kernel(steps, me, a, b, *refs):
    outs, held, sem = refs[-len(steps) - 2 : -2], refs[-2], refs[-1]
    y = lax.rem(me[0], LINE)
    pieces = []
    for d, out in zip(steps, outs):
        cols = group_cols(lax.rem(y + d, LINE))
        pieces.append((a.at[:, cols], len(pieces), out.at[0]))
        pieces.append((b.at[:, cols], len(pieces), out.at[1]))
    through(pieces, held, sem)


def pack(steps, me, a, b, *after, limit=60):
    n = len(steps)
    return pl.pallas_call(
        functools.partial(pack_kernel, steps),
        out_shape=(jax.ShapeDtypeStruct((2, a.shape[0], GW), BF),) * n,
        in_specs=[SMEM] + [ANY] * (2 + len(after)),
        out_specs=(ANY,) * n,
        scratch_shapes=[pltpu.VMEM((2 * n, a.shape[0], GW), BF), pltpu.SemaphoreType.DMA((2, 2 * n))],
        compiler_params=pltpu.CompilerParams(vmem_limit_bytes=limit * MIB),
        cost_estimate=TINY,
        name="pack",
    )(me, a, b, *after)


def load_kernel(place, v, a, after, v_own, v_other, a_own, a_send, held, sem):
    width = v_own.shape[1]
    rows = held.shape[1]
    own = pl.ds(pl.multiple_of(place[1] * width, HD), width)
    other = pl.ds(pl.multiple_of((1 - place[1]) * width, HD), width)
    whole = [
        pltpu.make_async_copy(a.at[:, own], a_own, sem.at[2, 0]),
        pltpu.make_async_copy(v.at[:, other], v_other, sem.at[2, 1]),
        pltpu.make_async_copy(v.at[:, own], v_own, sem.at[2, 2]),
    ]
    through([(a.at[pl.ds(i * rows, rows), other], i, a_send.at[pl.ds(i * rows, rows)]) for i in range(4)], held, sem)
    for copy in whole:
        copy.start()
    for copy in whole:
        copy.wait()


def load_projections(place, v, a, after):
    rows, width = v.shape[0], v.shape[1] // 2
    half = jax.ShapeDtypeStruct((rows, width), BF)
    return pl.pallas_call(
        load_kernel,
        out_shape=(half,) * 4,
        in_specs=[SMEM, ANY, ANY, ANY],
        out_specs=(VMEM, VMEM, VMEM, ANY),
        scratch_shapes=[pltpu.VMEM((4, rows // 4, width), BF), pltpu.SemaphoreType.DMA((3, 4))],
        compiler_params=pltpu.CompilerParams(vmem_limit_bytes=46 * MIB),
        cost_estimate=cost(6),
        name="load_projections",
    )(place, v, a, after)


def line_kernel(me, k, v, kv1, kv2, kv3, low, high, held, sem):
    y = lax.rem(me[0], LINE)
    cols = group_cols(y)
    copies = [
        pltpu.make_async_copy(k.at[:, cols], held.at[y, 0], sem.at[0]),
        pltpu.make_async_copy(v.at[:, cols], held.at[y, 1], sem.at[4]),
    ]
    for d, got in ((1, kv1), (2, kv2), (3, kv3)):
        copies.append(pltpu.make_async_copy(got, held.at[lax.rem(y + LINE - d, LINE)], sem.at[d]))
    for copy in copies:
        copy.start()
    for copy in copies:
        copy.wait()
    copies = [
        pltpu.make_async_copy(held.at[pl.ds(0, 2)], low, sem.at[0]),
        pltpu.make_async_copy(held.at[pl.ds(2, 2)], high, sem.at[1]),
    ]
    for copy in copies:
        copy.start()
    for copy in copies:
        copy.wait()


def line_blocks(me, k, v, kv1, kv2, kv3):
    half = jax.ShapeDtypeStruct((2, 2, AUD, GW), BF)
    return pl.pallas_call(
        line_kernel,
        out_shape=(half, half),
        in_specs=[SMEM] + [ANY] * 5,
        out_specs=(ANY, ANY),
        scratch_shapes=[pltpu.VMEM((LINE, 2, AUD, GW), BF), pltpu.SemaphoreType.DMA((5,))],
        compiler_params=pltpu.CompilerParams(vmem_limit_bytes=16 * MIB),
        cost_estimate=TINY,
        name="line_blocks",
    )(me, k, v, kv1, kv2, kv3)


def attend_kernel(steps, own, carried, last, *refs):
    refs = list(refs)

    def take(n):
        part = refs[:n]
        del refs[:n]
        return part

    me, first, count = take(3)
    kvs = [] if carried else take(4)
    q_own, v_own = take(2) if own else (None, None)
    arrived = take(len(steps) - (1 if own else 0))
    if carried:
        (kbuf,) = take(1)
        take(2)
    outs = take(len(steps))
    ubuf, csum = take(2)
    if not carried:
        (kbuf,) = take(1)
    if last:
        before, after = take(2)
    qbuf, obuf, tbuf, mbuf, cbuf, abuf, vtbuf, sem, qsem = refs

    y = lax.rem(me[0], LINE)
    base = me[0] - y
    copies = []

    def copy(src, dst):
        copies.append(pltpu.make_async_copy(src, dst, sem.at[len(copies)]))

    for i, part in enumerate(kvs):
        copy(part, kbuf.at[pl.ds(2 * i, 2)])
    if own:
        copy(q_own.at[:, group_cols(y)], qbuf.at[0, 0])
        copy(v_own.at[:, group_cols(y)], qbuf.at[0, 1])
    for c in copies:
        c.start()
    for i, part in enumerate(arrived):
        pltpu.make_async_copy(part, qbuf.at[i], qsem.at[i]).start()
    if not carried:
        csum[...] = jnp.full_like(csum, NEG)
    for c in copies:
        c.wait()

    def video(i, carry):
        if not own:
            pltpu.make_async_copy(qbuf.at[i], qbuf.at[i], qsem.at[i]).wait()
        step = jnp.int32(steps[0])
        for n in range(1, len(steps)):
            step = jnp.where(i == n, steps[n], step)
        v = lax.rem(y + LINE - step, LINE)
        lo = first[base + v] - base + 2
        hi = lo + count[base + v]
        mbuf[...] = jnp.full_like(mbuf, NEG)

        def scores(a, carry):
            slot = a - lo
            for h in range(GH):
                cols = slice(h * HD, (h + 1) * HD)
                t = lax.dot_general(
                    qbuf[i, 0, :, cols], kbuf[a, 0, :, cols], (((1,), (1,)), ((), ())), preferred_element_type=F32
                )
                t = t * SCALE
                tbuf[h, slot] = t
                mbuf[h] = jnp.maximum(mbuf[h], jnp.maximum(t[:, :HD], t[:, HD:]))
                cbuf[h, slot] = jnp.broadcast_to(jnp.max(t, axis=0, keepdims=True), (8, AUD))
            return carry

        lax.fori_loop(lo, hi, scores, 0)
        for h in range(GH):
            cols = slice(h * HD, (h + 1) * HD)
            mbuf[h] = jnp.broadcast_to(jnp.max(mbuf[h], axis=1, keepdims=True), (VID, HD))
            abuf[h] = jnp.zeros((VID, 2 * HD), F32)
            vtbuf[h, :HD] = qbuf[i, 1, :, cols].T
            vtbuf[h, HD:] = jnp.ones((EXTRA, VID), BF)

        def weights(a, carry):
            slot = a - lo
            for h in range(GH):
                cols = slice(h * HD, (h + 1) * HD)
                t = tbuf[h, slot]
                r = mbuf[h]
                c = cbuf[h, slot, 0:1]
                by_row = jnp.exp2(t - jnp.concatenate([r, r], axis=1)).astype(BF)
                values = jnp.concatenate([kbuf[a, 1, :, cols], jnp.ones((AUD, HD), BF)], axis=1)
                abuf[h] += jnp.dot(by_row, values, preferred_element_type=F32)
                by_col = jnp.exp2(t - c).astype(BF)
                u = jnp.dot(vtbuf[h], by_col, preferred_element_type=F32)
                old = csum[h, a, 0:1]
                new = jnp.maximum(old, c)
                kept = jnp.where(old > NEG, ubuf[h, a], 0.0)
                ubuf[h, a] = kept * jnp.exp2(old - new) + u * jnp.exp2(c - new)
                csum[h, a] = jnp.broadcast_to(new, (8, AUD))
            return carry

        lax.fori_loop(lo, hi, weights, 0)
        for h in range(GH):
            obuf[i, :, h * HD : (h + 1) * HD] = (abuf[h, :, :HD] / abuf[h, :, HD:]).astype(BF)
        return carry

    lax.fori_loop(0, len(steps), video, 0)

    copies = [pltpu.make_async_copy(obuf.at[i], out, sem.at[i]) for i, out in enumerate(outs)]
    for c in copies:
        c.start()
    if last:
        row = lax.broadcasted_iota(jnp.int32, (EXTRA, AUD), 0)
        for place, out in ((0, before), (6, after)):
            for j in range(2):
                for h in range(GH):
                    top = csum[h, place + j, 0:1]
                    some = top > NEG
                    n = jnp.where(some, ubuf[h, place + j, HD : HD + 1], 1.0)
                    u = jnp.where(some, ubuf[h, place + j, :HD], 0.0)
                    out[j, h, :HD] = (u / n).astype(BF)
                    level = jnp.where(some, top + jnp.log2(n), NEG)
                    hi = level.astype(BF).astype(F32)
                    mid = (level - hi).astype(BF).astype(F32)
                    lo = level - hi - mid
                    parts = jnp.where(row == 0, hi, jnp.where(row == 1, mid, jnp.where(row == 2, lo, 0.0)))
                    out[j, h, HD:] = parts.astype(BF)
    for c in copies:
        c.wait()


def attend(steps, info, kvs, own, arrived, sums, last):
    n = len(steps)
    n_idx = 2 * LINE
    sum_shapes = [
        jax.ShapeDtypeStruct((GH, n_idx, HD + EXTRA, AUD), F32),
        jax.ShapeDtypeStruct((GH, n_idx, 8, AUD), F32),
    ]
    out_shape = [jax.ShapeDtypeStruct((VID, GW), BF)] * n + sum_shapes
    out_specs = [ANY] * n + [VMEM] * 2
    if last:
        out_shape += [jax.ShapeDtypeStruct((2, GH, HD + EXTRA, AUD), BF)] * 2
        out_specs += [VMEM] * 2
    assert bool(own) != bool(sums)
    operands = [*info, *kvs, *own, *arrived, *sums]
    at = len(operands) - len(sums)
    if not sums:
        out_shape.append(jax.ShapeDtypeStruct((n_idx, 2, AUD, GW), BF))
        out_specs.append(VMEM)
    return pl.pallas_call(
        functools.partial(attend_kernel, steps, bool(own), bool(sums), last),
        out_shape=tuple(out_shape),
        in_specs=[SMEM] * 3 + [ANY] * (at - 3) + [VMEM] * len(sums),
        out_specs=tuple(out_specs),
        scratch_shapes=[
            pltpu.VMEM((n, 2, VID, GW), BF),
            pltpu.VMEM((n, VID, GW), BF),
            pltpu.VMEM((GH, 5, VID, AUD), F32),
            pltpu.VMEM((GH, VID, HD), F32),
            pltpu.VMEM((GH, 5, 8, AUD), F32),
            pltpu.VMEM((GH, VID, 2 * HD), F32),
            pltpu.VMEM((GH, HD + EXTRA, VID), BF),
            pltpu.SemaphoreType.DMA((8,)),
            pltpu.SemaphoreType.DMA((2,)),
        ],
        input_output_aliases={at + 1: n, at + 2: n + 1} if sums else {},
        compiler_params=pltpu.CompilerParams(vmem_limit_bytes=24 * MIB),
        cost_estimate=cost(6 * n),
        name="attend_last" if last else "attend",
    )(*operands)


def merge_kernel(me, u, c, prev, nxt, out0, out1, out2, out3):
    y = lax.rem(me[0], LINE)
    for d, out in enumerate((out0, out1, out2, out3)):
        j = lax.rem(y + d, LINE)
        for h in range(GH):
            low = j < 2
            at = lax.rem(j, 2)
            got = jnp.where(low, prev[at, h].astype(F32), nxt[at, h].astype(F32))
            level = got[HD : HD + 1] + got[HD + 1 : HD + 2] + got[HD + 2 : HD + 3]
            n = u[h, j + 2, HD : HD + 1]
            own = c[h, j + 2, 0:1] + jnp.log2(n)
            top = jnp.maximum(own, level)
            own_w = jnp.exp2(own - top)
            got_w = jnp.exp2(level - top)
            total = own_w + got_w
            mixed = u[h, j + 2, :HD] * (own_w / (n * total)) + got[:HD] * (got_w / total)
            out[:, h * HD : (h + 1) * HD] = mixed.T.astype(BF)


def merge(me, u, c, prev, nxt):
    return pl.pallas_call(
        merge_kernel,
        out_shape=(jax.ShapeDtypeStruct((AUD, GW), BF),) * LINE,
        in_specs=[SMEM] + [VMEM] * 4,
        out_specs=(VMEM,) * LINE,
        name="merge",
        cost_estimate=TINY,
        compiler_params=pltpu.CompilerParams(vmem_limit_bytes=24 * MIB),
    )(me, u, c, prev, nxt)


def near_kernel(place, o0, o1, o3, w_own, w_other, own, other, held, sem):
    y = place[0]
    copies = [pltpu.make_async_copy(o, held.at[i], sem.at[i]) for i, o in enumerate((o0, o1, o3))]
    for copy in copies:
        copy.start()
    for copy in copies:
        copy.wait()
    for w, out in ((w_other, other), (w_own, own)):
        for i, d in enumerate((0, 1, 3)):
            rows = group_cols(lax.rem(y + d, LINE))
            part = jnp.dot(held[i], w[rows, :], preferred_element_type=F32)
            out[...] = part if i == 0 else out[...] + part


def project_near(place, near, w_own, w_other):
    rows, width = near[0].shape[0], w_own.shape[1]
    return pl.pallas_call(
        near_kernel,
        out_shape=(jax.ShapeDtypeStruct((rows, width), F32),) * 2,
        in_specs=[SMEM] + [ANY] * 3 + [VMEM] * 2,
        out_specs=(VMEM,) * 2,
        scratch_shapes=[pltpu.VMEM((3, rows, GW), BF), pltpu.SemaphoreType.DMA((3,))],
        compiler_params=pltpu.CompilerParams(vmem_limit_bytes=16 * MIB),
        cost_estimate=cost(4),
        name="project_near",
    )(place, *near, w_own, w_other)


def far_kernel(n_add, place, piece, w, *refs):
    adds = refs[:n_add]
    out, held, sums, done, sem = refs[-5:]
    base, received = adds[0], adds[1:]
    tiles, _, tile = done.shape
    copies = [pltpu.make_async_copy(piece, held, sem.at[0, 0])]
    if received:
        copies.append(pltpu.make_async_copy(received[0], sums, sem.at[0, 1]))
    for copy in copies:
        copy.start()
    for copy in copies:
        copy.wait()
    rows = group_cols(lax.rem(place[0] + 2, LINE))
    outs = []
    for n in range(tiles):
        cols = slice(n * tile, (n + 1) * tile)
        total = base[:, cols] + jnp.dot(held[...], w[rows, cols], preferred_element_type=F32)
        if received:
            total += sums[:, cols].astype(F32)
        done[n] = total.astype(BF)
        outs.append(pltpu.make_async_copy(done.at[n], out.at[:, pl.ds(n * tile, tile)], sem.at[1, n]))
        outs[-1].start()
    for copy in outs:
        copy.wait()


def project_far(place, piece, w, base, received=(), after=()):
    rows, width = piece.shape[0], w.shape[1]
    tile = 384
    return pl.pallas_call(
        functools.partial(far_kernel, 1 + len(received)),
        out_shape=jax.ShapeDtypeStruct((rows, width), BF),
        in_specs=[SMEM, ANY, VMEM, VMEM] + [ANY] * (len(received) + len(after)),
        out_specs=ANY,
        scratch_shapes=[
            pltpu.VMEM((rows, GW), BF),
            pltpu.VMEM((rows, width), BF),
            pltpu.VMEM((width // tile, rows, tile), BF),
            pltpu.SemaphoreType.DMA((2, 8)),
        ],
        compiler_params=pltpu.CompilerParams(vmem_limit_bytes=16 * MIB),
        cost_estimate=cost(1),
        name="project_far",
    )(place, piece, w, base, *received, *after)


def project_kernel(place, *refs):
    mine, theirs = refs[:LINE], refs[LINE : 2 * LINE]
    w_mine, w_theirs, out, left, right, held, sem = refs[2 * LINE :]
    y = place[0]
    tiles, _, tile = held.shape
    ins = []
    for d in range(LINE):
        cols = group_cols(lax.rem(y + d, LINE))
        ins.append(pltpu.make_async_copy(mine[d], left.at[:, cols], sem.at[0, d]))
        ins.append(pltpu.make_async_copy(theirs[d], right.at[:, cols], sem.at[1, d]))
    for copy in ins:
        copy.start()
    for copy in ins:
        copy.wait()
    outs = []
    for n in range(tiles):
        cols = slice(n * tile, (n + 1) * tile)
        total = jnp.dot(left[...], w_mine[:, cols], preferred_element_type=F32)
        total += jnp.dot(right[...], w_theirs[:, cols], preferred_element_type=F32)
        held[n] = total.astype(BF)
        outs.append(pltpu.make_async_copy(held.at[n], out.at[:, pl.ds(n * tile, tile)], sem.at[2, n]))
        outs[-1].start()
    for copy in outs:
        copy.wait()


def project(place, mine, theirs, w, w_theirs):
    rows, width = mine[0].shape[0], w.shape[1]
    tile = 256
    return pl.pallas_call(
        project_kernel,
        out_shape=jax.ShapeDtypeStruct((rows, width), BF),
        in_specs=[SMEM] + [ANY] * (2 * LINE) + [VMEM] * 2,
        out_specs=ANY,
        scratch_shapes=[
            pltpu.VMEM((rows, LINE * GW), BF),
            pltpu.VMEM((rows, LINE * GW), BF),
            pltpu.VMEM((width // tile, rows, tile), BF),
            pltpu.SemaphoreType.DMA((3, 8)),
        ],
        compiler_params=pltpu.CompilerParams(vmem_limit_bytes=16 * MIB),
        cost_estimate=cost(4),
        name="project",
    )(place, *mine, *theirs, w, w_theirs)


def shards(
    video_query, video_value, audio_key, audio_value, video_proj, audio_proj, pair_first, pair_count
):
    nblocks = lax.axis_size("seq")
    me = lax.axis_index("seq").astype(jnp.int32)
    core = lax.axis_index("head").astype(jnp.int32)
    me_arr = me[None]
    place = jnp.stack([lax.rem(me, LINE), core])

    def along_line(x, d):
        return lax.ppermute(
            x, "seq", [(s, s // LINE * LINE + (s + d) % LINE) for s in range(nblocks)]
        )

    def across_lines(x, d):
        return lax.ppermute(x, "seq", [(s, (s + d * LINE) % nblocks) for s in range(nblocks)])

    def swap(x):
        return lax.ppermute(x, "head", [(0, 1), (1, 0)])

    kv_out = pack((1, 2, 3), me_arr, audio_key, audio_value)
    kv = [along_line(piece, d + 1) for d, piece in enumerate(kv_out)]
    near1, near3 = pack((1, 3), me_arr, video_query, video_value, kv_out[0])
    qv1, qv3 = along_line(near1, 1), along_line(near3, 3)
    (far,) = pack((2,), me_arr, video_query, video_value, qv1, qv3, limit=32)
    qv2 = along_line(far, 2)
    v_own, v_other, a_own, a_send = load_projections(place, video_proj, audio_proj, kv[0])
    a_other = swap(a_send)
    low, high = line_blocks(me_arr, audio_key, audio_value, *kv)
    before, after = across_lines(high, 1), across_lines(low, -1)

    info = (me_arr, pair_first, pair_count)
    kvs = (before, low, high, after)
    o0, u, c, kv_all = attend((0,), info, kvs, (video_query, video_value), (), (), False)
    o1, o3, u, c = attend((1, 3), info, (), (), (qv1, qv3), (kv_all, u, c), False)
    o2, u, c, to_prev, to_next = attend((2,), info, (), (), (qv2,), (kv_all, u, c), True)
    from_next, from_prev = across_lines(to_prev, -1), across_lines(to_next, 1)

    v1, v3, v2 = along_line(o1, -1), along_line(o3, -3), along_line(o2, -2)
    base, base_other = project_near(place, (o0, v1, v3), v_own, v_other)
    m0, m1, m2, m3 = merge(me_arr, u, c, from_prev, from_next)
    given = project_far(place, v2, v_other, base_other, after=(m0,))
    video_out = project_far(place, v2, v_own, base, received=(swap(given),))

    a_mine = (m0, along_line(m3, 3), along_line(m2, 2), along_line(m1, 1))
    audio_out = project(place, a_mine, tuple(swap(m) for m in a_mine), a_own, a_other)
    return video_out, audio_out


def solution(mesh):
    in_specs = (
        P("seq", "head"),
        P("seq", "head"),
        P("seq", "head"),
        P("seq", "head"),
        P("head", None),
        P("head", None),
        P(),
        P(),
    )
    out_specs = (P("seq", "head"), P("seq", "head"))
    return jax.shard_map(shards, mesh=mesh, in_specs=in_specs, out_specs=out_specs, check_vma=False)
```

```python
import functools
import math

import jax
import jax.numpy as jnp
from jax import lax
from jax.experimental import pallas as pl
from jax.experimental.pallas import tpu as pltpu
from jax.sharding import PartitionSpec as P

HD = 128
LINE = 4
GH = 3
GW = GH * HD
VID = 512
AUD = 256
NEG = -1e30
SCALE = math.log2(math.e) / math.sqrt(HD)
EXTRA = 16
BF = jnp.bfloat16
F32 = jnp.float32
MIB = 2**20


def cost(us):
    return pl.CostEstimate(flops=int(us * 1e9), bytes_accessed=1000, transcendentals=0)


TINY = cost(0.001)
ANY = pl.BlockSpec(memory_space=pl.ANY)
SMEM = pl.BlockSpec(memory_space=pltpu.SMEM)
VMEM = pl.BlockSpec(memory_space=pltpu.VMEM)


def group_cols(g):
    return pl.ds(pl.multiple_of(g * GW, HD), GW)


def through(pieces, held, sem):
    ins = [pltpu.make_async_copy(src, held.at[at], sem.at[0, i]) for i, (src, at, _) in enumerate(pieces)]
    outs = [pltpu.make_async_copy(held.at[at], dst, sem.at[1, i]) for i, (_, at, dst) in enumerate(pieces)]
    for copy in ins:
        copy.start()
    for copy, out in zip(ins, outs):
        copy.wait()
        out.start()
    for copy in outs:
        copy.wait()


def pack_kernel(steps, me, a, b, *refs):
    outs, held, sem = refs[-len(steps) - 2 : -2], refs[-2], refs[-1]
    y = lax.rem(me[0], LINE)
    pieces = []
    for d, out in zip(steps, outs):
        cols = group_cols(lax.rem(y + d, LINE))
        pieces.append((a.at[:, cols], len(pieces), out.at[0]))
        pieces.append((b.at[:, cols], len(pieces), out.at[1]))
    through(pieces, held, sem)


def pack(steps, me, a, b, *after, limit=60):
    n = len(steps)
    return pl.pallas_call(
        functools.partial(pack_kernel, steps),
        out_shape=(jax.ShapeDtypeStruct((2, a.shape[0], GW), BF),) * n,
        in_specs=[SMEM] + [ANY] * (2 + len(after)),
        out_specs=(ANY,) * n,
        scratch_shapes=[pltpu.VMEM((2 * n, a.shape[0], GW), BF), pltpu.SemaphoreType.DMA((2, 2 * n))],
        compiler_params=pltpu.CompilerParams(vmem_limit_bytes=limit * MIB),
        cost_estimate=TINY,
        name="pack",
    )(me, a, b, *after)


def send_half_kernel(place, w, after, out, held, sem):
    width = out.shape[1]
    rows = held.shape[1]
    other = pl.ds(pl.multiple_of((1 - place[1]) * width, HD), width)
    through([(w.at[pl.ds(i * rows, rows), other], i, out.at[pl.ds(i * rows, rows)]) for i in range(4)], held, sem)


def half_to_send(place, w, after):
    rows, width = w.shape[0], w.shape[1] // 2
    return pl.pallas_call(
        send_half_kernel,
        out_shape=jax.ShapeDtypeStruct((rows, width), BF),
        in_specs=[SMEM, ANY, ANY],
        out_specs=ANY,
        scratch_shapes=[pltpu.VMEM((4, rows // 4, width), BF), pltpu.SemaphoreType.DMA((2, 4))],
        compiler_params=pltpu.CompilerParams(vmem_limit_bytes=60 * MIB),
        cost_estimate=cost(4),
        name="half_to_send",
    )(place, w, after)


def load_kernel(place, v, a, after, v_own, v_other, a_own, token, sem):
    width = v_own.shape[1]
    own = pl.ds(pl.multiple_of(place[1] * width, HD), width)
    other = pl.ds(pl.multiple_of((1 - place[1]) * width, HD), width)
    copies = [
        pltpu.make_async_copy(v.at[:, other], v_other, sem.at[0]),
        pltpu.make_async_copy(v.at[:, own], v_own, sem.at[1]),
        pltpu.make_async_copy(a.at[:, own], a_own, sem.at[2]),
    ]
    for copy in copies:
        copy.start()
    token[...] = jnp.zeros_like(token)
    for copy in copies:
        copy.wait()


def load_projections(place, v, a, after):
    rows, width = v.shape[0], v.shape[1] // 2
    half = jax.ShapeDtypeStruct((rows, width), BF)
    return pl.pallas_call(
        load_kernel,
        out_shape=(half,) * 3 + (jax.ShapeDtypeStruct((8, HD), F32),),
        in_specs=[SMEM, ANY, ANY, ANY],
        out_specs=(VMEM,) * 4,
        scratch_shapes=[pltpu.SemaphoreType.DMA((3,))],
        compiler_params=pltpu.CompilerParams(vmem_limit_bytes=44 * MIB),
        cost_estimate=cost(8),
        name="load_projections",
    )(place, v, a, after)


def line_kernel(me, k, v, kv1, kv2, kv3, after, low, high, held, sem):
    y = lax.rem(me[0], LINE)
    cols = group_cols(y)
    copies = [
        pltpu.make_async_copy(k.at[:, cols], held.at[y, 0], sem.at[0]),
        pltpu.make_async_copy(v.at[:, cols], held.at[y, 1], sem.at[4]),
    ]
    for d, got in ((1, kv1), (2, kv2), (3, kv3)):
        copies.append(pltpu.make_async_copy(got, held.at[lax.rem(y + LINE - d, LINE)], sem.at[d]))
    for copy in copies:
        copy.start()
    for copy in copies:
        copy.wait()
    copies = [
        pltpu.make_async_copy(held.at[pl.ds(0, 2)], low, sem.at[0]),
        pltpu.make_async_copy(held.at[pl.ds(2, 2)], high, sem.at[1]),
    ]
    for copy in copies:
        copy.start()
    for copy in copies:
        copy.wait()


def line_blocks(me, k, v, kv1, kv2, kv3, after):
    half = jax.ShapeDtypeStruct((2, 2, AUD, GW), BF)
    return pl.pallas_call(
        line_kernel,
        out_shape=(half, half),
        in_specs=[SMEM] + [ANY] * 6,
        out_specs=(ANY, ANY),
        scratch_shapes=[pltpu.VMEM((LINE, 2, AUD, GW), BF), pltpu.SemaphoreType.DMA((5,))],
        compiler_params=pltpu.CompilerParams(vmem_limit_bytes=16 * MIB),
        cost_estimate=TINY,
        name="line_blocks",
    )(me, k, v, kv1, kv2, kv3, after)


def attend_kernel(steps, own, carried, last, *refs):
    refs = list(refs)

    def take(n):
        part = refs[:n]
        del refs[:n]
        return part

    me, first, count = take(3)
    kvs = [] if carried else take(4)
    q_own, v_own, _, _ = take(4) if own else (None,) * 4
    arrived = take(len(steps) - (1 if own else 0))
    if carried:
        (kbuf,) = take(1)
        take(2)
    outs = take(len(steps))
    ubuf, csum = take(2)
    if not carried:
        (kbuf,) = take(1)
    if last:
        before, after = take(2)
    qbuf, obuf, tbuf, mbuf, cbuf, abuf, vtbuf, sem, qsem = refs

    y = lax.rem(me[0], LINE)
    base = me[0] - y
    copies = []

    def copy(src, dst):
        copies.append(pltpu.make_async_copy(src, dst, sem.at[len(copies)]))

    for i, part in enumerate(kvs):
        copy(part, kbuf.at[pl.ds(2 * i, 2)])
    if own:
        copy(q_own.at[:, group_cols(y)], qbuf.at[0, 0])
        copy(v_own.at[:, group_cols(y)], qbuf.at[0, 1])
    for c in copies:
        c.start()
    for i, part in enumerate(arrived):
        pltpu.make_async_copy(part, qbuf.at[i + (1 if own else 0)], qsem.at[i]).start()
    if not carried:
        csum[...] = jnp.full_like(csum, NEG)
    for c in copies:
        c.wait()

    def video(i, carry):
        if own:

            @pl.when(i > 0)
            def _():
                pltpu.make_async_copy(qbuf.at[i], qbuf.at[i], qsem.at[i - 1]).wait()

        else:
            pltpu.make_async_copy(qbuf.at[i], qbuf.at[i], qsem.at[i]).wait()
        step = jnp.int32(steps[0])
        for n in range(1, len(steps)):
            step = jnp.where(i == n, steps[n], step)
        v = lax.rem(y + LINE - step, LINE)
        lo = first[base + v] - base + 2
        hi = lo + count[base + v]
        mbuf[...] = jnp.full_like(mbuf, NEG)

        def scores(a, carry):
            slot = a - lo
            for h in range(GH):
                cols = slice(h * HD, (h + 1) * HD)
                t = lax.dot_general(
                    qbuf[i, 0, :, cols], kbuf[a, 0, :, cols], (((1,), (1,)), ((), ())), preferred_element_type=F32
                )
                t = t * SCALE
                tbuf[h, slot] = t
                mbuf[h] = jnp.maximum(mbuf[h], jnp.maximum(t[:, :HD], t[:, HD:]))
                cbuf[h, slot] = jnp.broadcast_to(jnp.max(t, axis=0, keepdims=True), (8, AUD))
            return carry

        lax.fori_loop(lo, hi, scores, 0)
        for h in range(GH):
            cols = slice(h * HD, (h + 1) * HD)
            mbuf[h] = jnp.broadcast_to(jnp.max(mbuf[h], axis=1, keepdims=True), (VID, HD))
            abuf[h] = jnp.zeros((VID, 2 * HD), F32)
            vtbuf[h, :HD] = qbuf[i, 1, :, cols].T
            vtbuf[h, HD:] = jnp.ones((EXTRA, VID), BF)

        def weights(a, carry):
            slot = a - lo
            for h in range(GH):
                cols = slice(h * HD, (h + 1) * HD)
                t = tbuf[h, slot]
                r = mbuf[h]
                c = cbuf[h, slot, 0:1]
                by_row = jnp.exp2(t - jnp.concatenate([r, r], axis=1)).astype(BF)
                values = jnp.concatenate([kbuf[a, 1, :, cols], jnp.ones((AUD, HD), BF)], axis=1)
                abuf[h] += jnp.dot(by_row, values, preferred_element_type=F32)
                by_col = jnp.exp2(t - c).astype(BF)
                u = jnp.dot(vtbuf[h], by_col, preferred_element_type=F32)
                old = csum[h, a, 0:1]
                new = jnp.maximum(old, c)
                kept = jnp.where(old > NEG, ubuf[h, a], 0.0)
                ubuf[h, a] = kept * jnp.exp2(old - new) + u * jnp.exp2(c - new)
                csum[h, a] = jnp.broadcast_to(new, (8, AUD))
            return carry

        lax.fori_loop(lo, hi, weights, 0)
        for h in range(GH):
            obuf[i, :, h * HD : (h + 1) * HD] = (abuf[h, :, :HD] / abuf[h, :, HD:]).astype(BF)
        return carry

    lax.fori_loop(0, len(steps), video, 0)

    copies = [pltpu.make_async_copy(obuf.at[i], out, sem.at[i]) for i, out in enumerate(outs)]
    for c in copies:
        c.start()
    if last:
        row = lax.broadcasted_iota(jnp.int32, (EXTRA, AUD), 0)
        for place, out in ((0, before), (6, after)):
            for j in range(2):
                for h in range(GH):
                    top = csum[h, place + j, 0:1]
                    some = top > NEG
                    n = jnp.where(some, ubuf[h, place + j, HD : HD + 1], 1.0)
                    u = jnp.where(some, ubuf[h, place + j, :HD], 0.0)
                    out[j, h, :HD] = (u / n).astype(BF)
                    level = jnp.where(some, top + jnp.log2(n), NEG)
                    hi = level.astype(BF).astype(F32)
                    mid = (level - hi).astype(BF).astype(F32)
                    lo = level - hi - mid
                    parts = jnp.where(row == 0, hi, jnp.where(row == 1, mid, jnp.where(row == 2, lo, 0.0)))
                    out[j, h, HD:] = parts.astype(BF)
    for c in copies:
        c.wait()


def attend(steps, info, kvs, own, arrived, sums, last):
    n = len(steps)
    n_idx = 2 * LINE
    sum_shapes = [
        jax.ShapeDtypeStruct((GH, n_idx, HD + EXTRA, AUD), F32),
        jax.ShapeDtypeStruct((GH, n_idx, 8, AUD), F32),
    ]
    out_shape = [jax.ShapeDtypeStruct((VID, GW), BF)] * n + sum_shapes
    out_specs = [ANY] * n + [VMEM] * 2
    if last:
        out_shape += [jax.ShapeDtypeStruct((2, GH, HD + EXTRA, AUD), BF)] * 2
        out_specs += [VMEM] * 2
    assert bool(own) != bool(sums)
    operands = [*info, *kvs, *own, *arrived, *sums]
    at = len(operands) - len(sums)
    if not sums:
        out_shape.append(jax.ShapeDtypeStruct((n_idx, 2, AUD, GW), BF))
        out_specs.append(VMEM)
    return pl.pallas_call(
        functools.partial(attend_kernel, steps, bool(own), bool(sums), last),
        out_shape=tuple(out_shape),
        in_specs=[SMEM] * 3 + [ANY] * (at - 3) + [VMEM] * len(sums),
        out_specs=tuple(out_specs),
        scratch_shapes=[
            pltpu.VMEM((n, 2, VID, GW), BF),
            pltpu.VMEM((n, VID, GW), BF),
            pltpu.VMEM((GH, 5, VID, AUD), F32),
            pltpu.VMEM((GH, VID, HD), F32),
            pltpu.VMEM((GH, 5, 8, AUD), F32),
            pltpu.VMEM((GH, VID, 2 * HD), F32),
            pltpu.VMEM((GH, HD + EXTRA, VID), BF),
            pltpu.SemaphoreType.DMA((8,)),
            pltpu.SemaphoreType.DMA((2,)),
        ],
        input_output_aliases={at + 1: n, at + 2: n + 1} if sums else {},
        compiler_params=pltpu.CompilerParams(vmem_limit_bytes=18 * MIB),
        cost_estimate=cost(6 * n),
        name="attend_last" if last else "attend",
    )(*operands)


def merge_kernel(me, u, c, prev, nxt, out0, out1, out2, out3):
    y = lax.rem(me[0], LINE)
    for d, out in enumerate((out0, out1, out2, out3)):
        j = lax.rem(y + d, LINE)
        for h in range(GH):
            low = j < 2
            at = lax.rem(j, 2)
            got = jnp.where(low, prev[at, h].astype(F32), nxt[at, h].astype(F32))
            level = got[HD : HD + 1] + got[HD + 1 : HD + 2] + got[HD + 2 : HD + 3]
            n = u[h, j + 2, HD : HD + 1]
            own = c[h, j + 2, 0:1] + jnp.log2(n)
            top = jnp.maximum(own, level)
            own_w = jnp.exp2(own - top)
            got_w = jnp.exp2(level - top)
            total = own_w + got_w
            mixed = u[h, j + 2, :HD] * (own_w / (n * total)) + got[:HD] * (got_w / total)
            out[:, h * HD : (h + 1) * HD] = mixed.T.astype(BF)


def merge(me, u, c, prev, nxt):
    return pl.pallas_call(
        merge_kernel,
        out_shape=(jax.ShapeDtypeStruct((AUD, GW), BF),) * LINE,
        in_specs=[SMEM] + [VMEM] * 4,
        out_specs=(VMEM,) * LINE,
        name="merge",
        cost_estimate=TINY,
        compiler_params=pltpu.CompilerParams(vmem_limit_bytes=12 * MIB),
    )(me, u, c, prev, nxt)


def near_kernel(place, o0, o1, o3, w_own, w_other, own, other, held, sem):
    y = place[0]
    copies = [pltpu.make_async_copy(o, held.at[i], sem.at[i]) for i, o in enumerate((o0, o1, o3))]
    for copy in copies:
        copy.start()
    for copy in copies:
        copy.wait()
    for w, out in ((w_other, other), (w_own, own)):
        for i, d in enumerate((0, 1, 3)):
            rows = group_cols(lax.rem(y + d, LINE))
            part = jnp.dot(held[i], w[rows, :], preferred_element_type=F32)
            out[...] = part if i == 0 else out[...] + part


def project_near(place, near, w_own, w_other):
    rows, width = near[0].shape[0], w_own.shape[1]
    return pl.pallas_call(
        near_kernel,
        out_shape=(jax.ShapeDtypeStruct((rows, width), F32),) * 2,
        in_specs=[SMEM] + [ANY] * 3 + [VMEM] * 2,
        out_specs=(VMEM,) * 2,
        scratch_shapes=[pltpu.VMEM((3, rows, GW), BF), pltpu.SemaphoreType.DMA((3,))],
        compiler_params=pltpu.CompilerParams(vmem_limit_bytes=16 * MIB),
        cost_estimate=cost(4),
        name="project_near",
    )(place, *near, w_own, w_other)


def far_kernel(n_add, place, piece, w, *refs):
    adds = refs[:n_add]
    out, held, sums, done, sem = refs[-5:]
    base, received = adds[0], adds[1:]
    tiles, _, tile = done.shape
    copies = [pltpu.make_async_copy(piece, held, sem.at[0, 0])]
    if received:
        copies.append(pltpu.make_async_copy(received[0], sums, sem.at[0, 1]))
    for copy in copies:
        copy.start()
    for copy in copies:
        copy.wait()
    rows = group_cols(lax.rem(place[0] + 2, LINE))
    outs = []
    for n in range(tiles):
        cols = slice(n * tile, (n + 1) * tile)
        total = base[:, cols] + jnp.dot(held[...], w[rows, cols], preferred_element_type=F32)
        if received:
            total += sums[:, cols].astype(F32)
        done[n] = total.astype(BF)
        outs.append(pltpu.make_async_copy(done.at[n], out.at[:, pl.ds(n * tile, tile)], sem.at[1, n]))
        outs[-1].start()
    for copy in outs:
        copy.wait()


def project_far(place, piece, w, base, received=(), after=()):
    rows, width = piece.shape[0], w.shape[1]
    tile = 384
    return pl.pallas_call(
        functools.partial(far_kernel, 1 + len(received)),
        out_shape=jax.ShapeDtypeStruct((rows, width), BF),
        in_specs=[SMEM, ANY, VMEM, VMEM] + [ANY] * (len(received) + len(after)),
        out_specs=ANY,
        scratch_shapes=[
            pltpu.VMEM((rows, GW), BF),
            pltpu.VMEM((rows, width), BF),
            pltpu.VMEM((width // tile, rows, tile), BF),
            pltpu.SemaphoreType.DMA((2, 8)),
        ],
        compiler_params=pltpu.CompilerParams(vmem_limit_bytes=16 * MIB),
        cost_estimate=cost(0.5),
        name="project_far",
    )(place, piece, w, base, *received, *after)


def project_kernel(place, *refs):
    mine, theirs = refs[:LINE], refs[LINE : 2 * LINE]
    w_mine, w_theirs, out, left, right, held, sem = refs[2 * LINE :]
    y = place[0]
    tiles, _, tile = held.shape
    ins = []
    for d in range(LINE):
        cols = group_cols(lax.rem(y + d, LINE))
        ins.append(pltpu.make_async_copy(mine[d], left.at[:, cols], sem.at[0, d]))
        ins.append(pltpu.make_async_copy(theirs[d], right.at[:, cols], sem.at[1, d]))
    for copy in ins:
        copy.start()
    for copy in ins:
        copy.wait()
    outs = []
    for n in range(tiles):
        cols = slice(n * tile, (n + 1) * tile)
        total = jnp.dot(left[...], w_mine[:, cols], preferred_element_type=F32)
        total += jnp.dot(right[...], w_theirs[:, cols], preferred_element_type=F32)
        held[n] = total.astype(BF)
        outs.append(pltpu.make_async_copy(held.at[n], out.at[:, pl.ds(n * tile, tile)], sem.at[2, n]))
        outs[-1].start()
    for copy in outs:
        copy.wait()


def project(place, mine, theirs, w, w_theirs):
    rows, width = mine[0].shape[0], w.shape[1]
    tile = 256
    return pl.pallas_call(
        project_kernel,
        out_shape=jax.ShapeDtypeStruct((rows, width), BF),
        in_specs=[SMEM] + [ANY] * (2 * LINE) + [VMEM] * 2,
        out_specs=ANY,
        scratch_shapes=[
            pltpu.VMEM((rows, LINE * GW), BF),
            pltpu.VMEM((rows, LINE * GW), BF),
            pltpu.VMEM((width // tile, rows, tile), BF),
            pltpu.SemaphoreType.DMA((3, 8)),
        ],
        compiler_params=pltpu.CompilerParams(vmem_limit_bytes=16 * MIB),
        cost_estimate=cost(4),
        name="project",
    )(place, *mine, *theirs, w, w_theirs)


def shards(
    video_query, video_value, audio_key, audio_value, video_proj, audio_proj, pair_first, pair_count
):
    nblocks = lax.axis_size("seq")
    me = lax.axis_index("seq").astype(jnp.int32)
    core = lax.axis_index("head").astype(jnp.int32)
    me_arr = me[None]
    place = jnp.stack([lax.rem(me, LINE), core])

    def along_line(x, d):
        return lax.ppermute(
            x, "seq", [(s, s // LINE * LINE + (s + d) % LINE) for s in range(nblocks)]
        )

    def across_lines(x, d):
        return lax.ppermute(x, "seq", [(s, (s + d * LINE) % nblocks) for s in range(nblocks)])

    def swap(x):
        return lax.ppermute(x, "head", [(0, 1), (1, 0)])

    kv_out = pack((1, 2, 3), me_arr, audio_key, audio_value)
    kv = [along_line(piece, d + 1) for d, piece in enumerate(kv_out)]
    near1, near3 = pack((1, 3), me_arr, video_query, video_value, kv_out[0])
    qv1, qv3 = along_line(near1, 1), along_line(near3, 3)
    a_send = half_to_send(place, audio_proj, near1)
    a_other = swap(a_send)
    low, high = line_blocks(me_arr, audio_key, audio_value, *kv, a_send)
    before, after = across_lines(high, 1), across_lines(low, -1)
    v_own, v_other, a_own, token = load_projections(place, video_proj, audio_proj, low)
    (far,) = pack((2,), me_arr, video_query, video_value, low, limit=32)
    qv2 = along_line(far, 2)

    info = (me_arr, pair_first, pair_count)
    kvs = (before, low, high, after)
    own = (video_query, video_value, far, token)
    o0, o1, o3, u, c, kv_all = attend((0, 1, 3), info, kvs, own, (qv1, qv3), (), False)
    o2, u, c, to_prev, to_next = attend((2,), info, (), (), (qv2,), (kv_all, u, c), True)
    from_next, from_prev = across_lines(to_prev, -1), across_lines(to_next, 1)

    v1, v3, v2 = along_line(o1, -1), along_line(o3, -3), along_line(o2, -2)
    base, base_other = project_near(place, (o0, v1, v3), v_own, v_other)
    m0, m1, m2, m3 = merge(me_arr, u, c, from_prev, from_next)
    given = project_far(place, v2, v_other, base_other, after=(m0,))
    video_out = project_far(place, v2, v_own, base, received=(swap(given),))

    a_mine = (m0, along_line(m3, 3), along_line(m2, 2), along_line(m1, 1))
    audio_out = project(place, a_mine, tuple(swap(m) for m in a_mine), a_own, a_other)
    return video_out, audio_out


def solution(mesh):
    in_specs = (
        P("seq", "head"),
        P("seq", "head"),
        P("seq", "head"),
        P("seq", "head"),
        P("head", None),
        P("head", None),
        P(),
        P(),
    )
    out_specs = (P("seq", "head"), P("seq", "head"))
    return jax.shard_map(shards, mesh=mesh, in_specs=in_specs, out_specs=out_specs, check_vma=False)
```

```python
import functools
import math

import jax
import jax.numpy as jnp
from jax import lax
from jax.experimental import pallas as pl
from jax.experimental.pallas import tpu as pltpu
from jax.sharding import PartitionSpec as P

HD = 128
LINE = 4
GH = 3
GW = GH * HD
VID = 512
AUD = 256
NEG = -1e30
SCALE = math.log2(math.e) / math.sqrt(HD)
EXTRA = 16
BF = jnp.bfloat16
F32 = jnp.float32
MIB = 2**20


def cost(us):
    return pl.CostEstimate(flops=int(us * 1e9), bytes_accessed=1000, transcendentals=0)


TINY = cost(0.001)
ANY = pl.BlockSpec(memory_space=pl.ANY)
SMEM = pl.BlockSpec(memory_space=pltpu.SMEM)
VMEM = pl.BlockSpec(memory_space=pltpu.VMEM)


def group_cols(g):
    return pl.ds(pl.multiple_of(g * GW, HD), GW)


def through(pieces, held, sem):
    ins = [pltpu.make_async_copy(src, held.at[at], sem.at[0, i]) for i, (src, at, _) in enumerate(pieces)]
    outs = [pltpu.make_async_copy(held.at[at], dst, sem.at[1, i]) for i, (_, at, dst) in enumerate(pieces)]
    for copy in ins:
        copy.start()
    for copy, out in zip(ins, outs):
        copy.wait()
        out.start()
    for copy in outs:
        copy.wait()


def pack_kernel(steps, me, a, b, *refs):
    outs, held, sem = refs[-len(steps) - 2 : -2], refs[-2], refs[-1]
    y = lax.rem(me[0], LINE)
    pieces = []
    for d, out in zip(steps, outs):
        cols = group_cols(lax.rem(y + d, LINE))
        pieces.append((a.at[:, cols], len(pieces), out.at[0]))
        pieces.append((b.at[:, cols], len(pieces), out.at[1]))
    through(pieces, held, sem)


def pack(steps, me, a, b, *after, limit=60):
    n = len(steps)
    return pl.pallas_call(
        functools.partial(pack_kernel, steps),
        out_shape=(jax.ShapeDtypeStruct((2, a.shape[0], GW), BF),) * n,
        in_specs=[SMEM] + [ANY] * (2 + len(after)),
        out_specs=(ANY,) * n,
        scratch_shapes=[pltpu.VMEM((2 * n, a.shape[0], GW), BF), pltpu.SemaphoreType.DMA((2, 2 * n))],
        compiler_params=pltpu.CompilerParams(vmem_limit_bytes=limit * MIB),
        cost_estimate=TINY,
        name="pack",
    )(me, a, b, *after)


def send_half_kernel(place, w, after, out, held, sem):
    width = out.shape[1]
    rows = held.shape[1]
    other = pl.ds(pl.multiple_of((1 - place[1]) * width, HD), width)
    through([(w.at[pl.ds(i * rows, rows), other], i, out.at[pl.ds(i * rows, rows)]) for i in range(4)], held, sem)


def half_to_send(place, w, after):
    rows, width = w.shape[0], w.shape[1] // 2
    return pl.pallas_call(
        send_half_kernel,
        out_shape=jax.ShapeDtypeStruct((rows, width), BF),
        in_specs=[SMEM, ANY, ANY],
        out_specs=ANY,
        scratch_shapes=[pltpu.VMEM((4, rows // 4, width), BF), pltpu.SemaphoreType.DMA((2, 4))],
        compiler_params=pltpu.CompilerParams(vmem_limit_bytes=60 * MIB),
        cost_estimate=cost(4),
        name="half_to_send",
    )(place, w, after)


def load_kernel(place, v, a, after, v_own, v_other, a_own, token, sem):
    width = v_own.shape[1]
    own = pl.ds(pl.multiple_of(place[1] * width, HD), width)
    other = pl.ds(pl.multiple_of((1 - place[1]) * width, HD), width)
    copies = [
        pltpu.make_async_copy(v.at[:, other], v_other, sem.at[0]),
        pltpu.make_async_copy(v.at[:, own], v_own, sem.at[1]),
        pltpu.make_async_copy(a.at[:, own], a_own, sem.at[2]),
    ]
    for copy in copies:
        copy.start()
    token[...] = jnp.zeros_like(token)
    for copy in copies:
        copy.wait()


def load_projections(place, v, a, after):
    rows, width = v.shape[0], v.shape[1] // 2
    half = jax.ShapeDtypeStruct((rows, width), BF)
    return pl.pallas_call(
        load_kernel,
        out_shape=(half,) * 3 + (jax.ShapeDtypeStruct((8, HD), F32),),
        in_specs=[SMEM, ANY, ANY, ANY],
        out_specs=(VMEM,) * 4,
        scratch_shapes=[pltpu.SemaphoreType.DMA((3,))],
        compiler_params=pltpu.CompilerParams(vmem_limit_bytes=44 * MIB),
        cost_estimate=cost(8),
        name="load_projections",
    )(place, v, a, after)


def line_kernel(me, k, v, kv1, kv2, kv3, after, low, high, held, sem):
    y = lax.rem(me[0], LINE)
    cols = group_cols(y)
    copies = [
        pltpu.make_async_copy(k.at[:, cols], held.at[y, 0], sem.at[0]),
        pltpu.make_async_copy(v.at[:, cols], held.at[y, 1], sem.at[4]),
    ]
    for d, got in ((1, kv1), (2, kv2), (3, kv3)):
        copies.append(pltpu.make_async_copy(got, held.at[lax.rem(y + LINE - d, LINE)], sem.at[d]))
    for copy in copies:
        copy.start()
    for copy in copies:
        copy.wait()
    copies = [
        pltpu.make_async_copy(held.at[pl.ds(0, 2)], low, sem.at[0]),
        pltpu.make_async_copy(held.at[pl.ds(2, 2)], high, sem.at[1]),
    ]
    for copy in copies:
        copy.start()
    for copy in copies:
        copy.wait()


def line_blocks(me, k, v, kv1, kv2, kv3, after):
    half = jax.ShapeDtypeStruct((2, 2, AUD, GW), BF)
    return pl.pallas_call(
        line_kernel,
        out_shape=(half, half),
        in_specs=[SMEM] + [ANY] * 6,
        out_specs=(ANY, ANY),
        scratch_shapes=[pltpu.VMEM((LINE, 2, AUD, GW), BF), pltpu.SemaphoreType.DMA((5,))],
        compiler_params=pltpu.CompilerParams(vmem_limit_bytes=16 * MIB),
        cost_estimate=TINY,
        name="line_blocks",
    )(me, k, v, kv1, kv2, kv3, after)


def attend_kernel(steps, own, carried, last, *refs):
    refs = list(refs)

    def take(n):
        part = refs[:n]
        del refs[:n]
        return part

    me, first, count = take(3)
    kvs = [] if carried else take(4)
    q_own, v_own, _, _ = take(4) if own else (None,) * 4
    arrived = take(len(steps) - (1 if own else 0))
    if carried:
        (kbuf,) = take(1)
        take(2)
    outs = take(len(steps))
    ubuf, csum = take(2)
    if not carried:
        (kbuf,) = take(1)
    if last:
        before, after = take(2)
    qbuf, tbuf, mbuf, cbuf, abuf, vtbuf, sem, qsem = refs

    y = lax.rem(me[0], LINE)
    base = me[0] - y
    copies = []

    def copy(src, dst):
        copies.append(pltpu.make_async_copy(src, dst, sem.at[len(copies)]))

    for i, part in enumerate(kvs):
        copy(part, kbuf.at[pl.ds(2 * i, 2)])
    if own:
        copy(q_own.at[:, group_cols(y)], qbuf.at[0, 0])
        copy(v_own.at[:, group_cols(y)], qbuf.at[0, 1])
    for c in copies:
        c.start()
    for i, part in enumerate(arrived):
        pltpu.make_async_copy(part, qbuf.at[i + (1 if own else 0)], qsem.at[i]).start()
    if not carried:
        csum[...] = jnp.full_like(csum, NEG)
    for c in copies:
        c.wait()

    diagonal = lax.broadcasted_iota(jnp.int32, (HD, HD), 0) == lax.broadcasted_iota(jnp.int32, (HD, HD), 1)
    unit = jnp.where(diagonal, 1.0, 0.0).astype(BF)

    def video(i, carry):
        if own:

            @pl.when(i > 0)
            def _():
                pltpu.make_async_copy(qbuf.at[i], qbuf.at[i], qsem.at[i - 1]).wait()

        else:
            pltpu.make_async_copy(qbuf.at[i], qbuf.at[i], qsem.at[i]).wait()
        step = jnp.int32(steps[0])
        for n in range(1, len(steps)):
            step = jnp.where(i == n, steps[n], step)
        v = lax.rem(y + LINE - step, LINE)
        lo = first[base + v] - base + 2
        hi = lo + count[base + v]
        def scores(a, carry):
            slot = a - lo
            for h in range(GH):
                cols = slice(h * HD, (h + 1) * HD)
                t = lax.dot_general(
                    qbuf[i, 0, :, cols], kbuf[a, 0, :, cols], (((1,), (1,)), ((), ())), preferred_element_type=F32
                )
                t = t * SCALE
                tbuf[h, slot] = t
                top = jnp.maximum(t[:, :HD], t[:, HD:])
                mbuf[h] = jnp.where(slot == 0, top, jnp.maximum(mbuf[h], top))
                cbuf[h, slot] = jnp.broadcast_to(jnp.max(t, axis=0, keepdims=True), (8, AUD))
            return carry

        lax.fori_loop(lo, hi, scores, 0)
        for h in range(GH):
            cols = slice(h * HD, (h + 1) * HD)
            mbuf[h] = jnp.broadcast_to(jnp.max(mbuf[h], axis=1, keepdims=True), (VID, HD))
            abuf[h] = jnp.zeros((VID, 2 * HD), F32)
            turned = lax.dot_general(
                unit, qbuf[i, 1, :, cols], (((1,), (1,)), ((), ())), preferred_element_type=F32
            )
            vtbuf[h, :HD] = turned.astype(BF)
            vtbuf[h, HD:] = jnp.ones((EXTRA, VID), BF)

        def weights(a, carry):
            slot = a - lo
            for h in range(GH):
                cols = slice(h * HD, (h + 1) * HD)
                t = tbuf[h, slot]
                r = mbuf[h]
                c = cbuf[h, slot, 0:1]
                by_row = jnp.exp2(t - jnp.concatenate([r, r], axis=1)).astype(BF)
                values = jnp.concatenate([kbuf[a, 1, :, cols], jnp.ones((AUD, HD), BF)], axis=1)
                abuf[h] += jnp.dot(by_row, values, preferred_element_type=F32)
                by_col = jnp.exp2(t - c).astype(BF)
                u = jnp.dot(vtbuf[h], by_col, preferred_element_type=F32)
                old = csum[h, a, 0:1]
                new = jnp.maximum(old, c)
                kept = jnp.where(old > NEG, ubuf[h, a], 0.0)
                ubuf[h, a] = kept * jnp.exp2(old - new) + u * jnp.exp2(c - new)
                csum[h, a] = jnp.broadcast_to(new, (8, AUD))
            return carry

        lax.fori_loop(lo, hi, weights, 0)
        for n, out in enumerate(outs):

            @pl.when(i == n)
            def _():
                for h in range(GH):
                    out[:, h * HD : (h + 1) * HD] = (abuf[h, :, :HD] / abuf[h, :, HD:]).astype(BF)

        return carry

    lax.fori_loop(0, len(steps), video, 0)

    if last:
        row = lax.broadcasted_iota(jnp.int32, (EXTRA, AUD), 0)
        for place, out in ((0, before), (6, after)):
            for j in range(2):
                for h in range(GH):
                    top = csum[h, place + j, 0:1]
                    some = top > NEG
                    n = jnp.where(some, ubuf[h, place + j, HD : HD + 1], 1.0)
                    u = jnp.where(some, ubuf[h, place + j, :HD], 0.0)
                    out[j, h, :HD] = (u / n).astype(BF)
                    level = jnp.where(some, top + jnp.log2(n), NEG)
                    hi = level.astype(BF).astype(F32)
                    mid = (level - hi).astype(BF).astype(F32)
                    lo = level - hi - mid
                    parts = jnp.where(row == 0, hi, jnp.where(row == 1, mid, jnp.where(row == 2, lo, 0.0)))
                    out[j, h, HD:] = parts.astype(BF)


def attend(steps, info, kvs, own, arrived, sums, last):
    n = len(steps)
    n_idx = 2 * LINE
    sum_shapes = [
        jax.ShapeDtypeStruct((GH, n_idx, HD + EXTRA, AUD), F32),
        jax.ShapeDtypeStruct((GH, n_idx, 8, AUD), F32),
    ]
    out_shape = [jax.ShapeDtypeStruct((VID, GW), BF)] * n + sum_shapes
    out_specs = [VMEM] * (n + 2)
    if last:
        out_shape += [jax.ShapeDtypeStruct((2, GH, HD + EXTRA, AUD), BF)] * 2
        out_specs += [VMEM] * 2
    assert bool(own) != bool(sums)
    operands = [*info, *kvs, *own, *arrived, *sums]
    at = len(operands) - len(sums)
    if not sums:
        out_shape.append(jax.ShapeDtypeStruct((n_idx, 2, AUD, GW), BF))
        out_specs.append(VMEM)
    return pl.pallas_call(
        functools.partial(attend_kernel, steps, bool(own), bool(sums), last),
        out_shape=tuple(out_shape),
        in_specs=[SMEM] * 3 + [ANY] * (at - 3) + [VMEM] * len(sums),
        out_specs=tuple(out_specs),
        scratch_shapes=[
            pltpu.VMEM((n, 2, VID, GW), BF),
            pltpu.VMEM((GH, 5, VID, AUD), F32),
            pltpu.VMEM((GH, VID, HD), F32),
            pltpu.VMEM((GH, 5, 8, AUD), F32),
            pltpu.VMEM((GH, VID, 2 * HD), F32),
            pltpu.VMEM((GH, HD + EXTRA, VID), BF),
            pltpu.SemaphoreType.DMA((8,)),
            pltpu.SemaphoreType.DMA((2,)),
        ],
        input_output_aliases={at + 1: n, at + 2: n + 1} if sums else {},
        compiler_params=pltpu.CompilerParams(vmem_limit_bytes=18 * MIB),
        cost_estimate=cost(6 * n),
        name="attend_last" if last else "attend",
    )(*operands)


def merge_kernel(me, u, c, prev, nxt, out0, out1, out2, out3):
    y = lax.rem(me[0], LINE)
    for d, out in enumerate((out0, out1, out2, out3)):
        j = lax.rem(y + d, LINE)
        for h in range(GH):
            low = j < 2
            at = lax.rem(j, 2)
            got = jnp.where(low, prev[at, h].astype(F32), nxt[at, h].astype(F32))
            level = got[HD : HD + 1] + got[HD + 1 : HD + 2] + got[HD + 2 : HD + 3]
            n = u[h, j + 2, HD : HD + 1]
            own = c[h, j + 2, 0:1] + jnp.log2(n)
            top = jnp.maximum(own, level)
            own_w = jnp.exp2(own - top)
            got_w = jnp.exp2(level - top)
            total = own_w + got_w
            mixed = u[h, j + 2, :HD] * (own_w / (n * total)) + got[:HD] * (got_w / total)
            out[:, h * HD : (h + 1) * HD] = mixed.T.astype(BF)


def merge(me, u, c, prev, nxt):
    return pl.pallas_call(
        merge_kernel,
        out_shape=(jax.ShapeDtypeStruct((AUD, GW), BF),) * LINE,
        in_specs=[SMEM] + [VMEM] * 4,
        out_specs=(VMEM,) * LINE,
        name="merge",
        cost_estimate=TINY,
        compiler_params=pltpu.CompilerParams(vmem_limit_bytes=12 * MIB),
    )(me, u, c, prev, nxt)


def near_kernel(place, o0, o1, o3, w_own, w_other, own, other, held, sem):
    y = place[0]
    copies = [pltpu.make_async_copy(o, held.at[i], sem.at[i]) for i, o in enumerate((o0, o1, o3))]
    for copy in copies:
        copy.start()
    for copy in copies:
        copy.wait()
    for w, out in ((w_other, other), (w_own, own)):
        for i, d in enumerate((0, 1, 3)):
            rows = group_cols(lax.rem(y + d, LINE))
            part = jnp.dot(held[i], w[rows, :], preferred_element_type=F32)
            out[...] = part if i == 0 else out[...] + part


def project_near(place, near, w_own, w_other):
    rows, width = near[0].shape[0], w_own.shape[1]
    return pl.pallas_call(
        near_kernel,
        out_shape=(jax.ShapeDtypeStruct((rows, width), F32),) * 2,
        in_specs=[SMEM] + [ANY] * 3 + [VMEM] * 2,
        out_specs=(VMEM,) * 2,
        scratch_shapes=[pltpu.VMEM((3, rows, GW), BF), pltpu.SemaphoreType.DMA((3,))],
        compiler_params=pltpu.CompilerParams(vmem_limit_bytes=16 * MIB),
        cost_estimate=cost(4),
        name="project_near",
    )(place, *near, w_own, w_other)


def far_kernel(n_add, place, piece, w, *refs):
    adds = refs[:n_add]
    out, done, sem = refs[-3:]
    base, received = adds[0], adds[1:]
    tiles, _, tile = done.shape
    rows = group_cols(lax.rem(place[0] + 2, LINE))
    outs = []
    for n in range(tiles):
        cols = slice(n * tile, (n + 1) * tile)
        total = base[:, cols] + jnp.dot(piece[...], w[rows, cols], preferred_element_type=F32)
        if received:
            total += received[0][:, cols].astype(F32)
        if not received:
            out[:, cols] = total.astype(BF)
            continue
        done[n] = total.astype(BF)
        outs.append(pltpu.make_async_copy(done.at[n], out.at[:, pl.ds(n * tile, tile)], sem.at[n]))
        outs[-1].start()
    for copy in outs:
        copy.wait()


def project_far(place, piece, w, base, received=(), after=()):
    rows, width = piece.shape[0], w.shape[1]
    tile = 384
    return pl.pallas_call(
        functools.partial(far_kernel, 1 + len(received)),
        out_shape=jax.ShapeDtypeStruct((rows, width), BF),
        in_specs=[SMEM, VMEM, VMEM, VMEM] + [VMEM] * len(received) + [ANY] * len(after),
        out_specs=ANY if received else VMEM,
        scratch_shapes=[
            pltpu.VMEM((width // tile, rows, tile), BF),
            pltpu.SemaphoreType.DMA((8,)),
        ],
        compiler_params=pltpu.CompilerParams(vmem_limit_bytes=16 * MIB),
        cost_estimate=cost(0.5),
        name="project_far",
    )(place, piece, w, base, *received, *after)


def project_kernel(place, *refs):
    mine, theirs = refs[:LINE], refs[LINE : 2 * LINE]
    w_mine, w_theirs, out, left, right, held, sem = refs[2 * LINE :]
    y = place[0]
    tiles, _, tile = held.shape
    ins = []
    for d in range(LINE):
        cols = group_cols(lax.rem(y + d, LINE))
        ins.append(pltpu.make_async_copy(mine[d], left.at[:, cols], sem.at[0, d]))
        ins.append(pltpu.make_async_copy(theirs[d], right.at[:, cols], sem.at[1, d]))
    for copy in ins:
        copy.start()
    for copy in ins:
        copy.wait()
    outs = []
    for n in range(tiles):
        cols = slice(n * tile, (n + 1) * tile)
        total = jnp.dot(left[...], w_mine[:, cols], preferred_element_type=F32)
        total += jnp.dot(right[...], w_theirs[:, cols], preferred_element_type=F32)
        held[n] = total.astype(BF)
        outs.append(pltpu.make_async_copy(held.at[n], out.at[:, pl.ds(n * tile, tile)], sem.at[2, n]))
        outs[-1].start()
    for copy in outs:
        copy.wait()


def project(place, mine, theirs, w, w_theirs):
    rows, width = mine[0].shape[0], w.shape[1]
    tile = 256
    return pl.pallas_call(
        project_kernel,
        out_shape=jax.ShapeDtypeStruct((rows, width), BF),
        in_specs=[SMEM] + [ANY] * (2 * LINE) + [VMEM] * 2,
        out_specs=ANY,
        scratch_shapes=[
            pltpu.VMEM((rows, LINE * GW), BF),
            pltpu.VMEM((rows, LINE * GW), BF),
            pltpu.VMEM((width // tile, rows, tile), BF),
            pltpu.SemaphoreType.DMA((3, 8)),
        ],
        compiler_params=pltpu.CompilerParams(vmem_limit_bytes=16 * MIB),
        cost_estimate=cost(4),
        name="project",
    )(place, *mine, *theirs, w, w_theirs)


def shards(
    video_query, video_value, audio_key, audio_value, video_proj, audio_proj, pair_first, pair_count
):
    nblocks = lax.axis_size("seq")
    me = lax.axis_index("seq").astype(jnp.int32)
    core = lax.axis_index("head").astype(jnp.int32)
    me_arr = me[None]
    place = jnp.stack([lax.rem(me, LINE), core])

    def along_line(x, d):
        return lax.ppermute(
            x, "seq", [(s, s // LINE * LINE + (s + d) % LINE) for s in range(nblocks)]
        )

    def across_lines(x, d):
        return lax.ppermute(x, "seq", [(s, (s + d * LINE) % nblocks) for s in range(nblocks)])

    def swap(x):
        return lax.ppermute(x, "head", [(0, 1), (1, 0)])

    kv_out = pack((1, 2, 3), me_arr, audio_key, audio_value)
    kv = [along_line(piece, d + 1) for d, piece in enumerate(kv_out)]
    near1, near3 = pack((1, 3), me_arr, video_query, video_value, kv_out[0])
    qv1, qv3 = along_line(near1, 1), along_line(near3, 3)
    a_send = half_to_send(place, audio_proj, near1)
    a_other = swap(a_send)
    low, high = line_blocks(me_arr, audio_key, audio_value, *kv, a_send)
    before, after = across_lines(high, 1), across_lines(low, -1)
    v_own, v_other, a_own, token = load_projections(place, video_proj, audio_proj, low)
    (far,) = pack((2,), me_arr, video_query, video_value, low, limit=32)
    qv2 = along_line(far, 2)

    info = (me_arr, pair_first, pair_count)
    kvs = (before, low, high, after)
    own = (video_query, video_value, far, token)
    o0, o1, o3, u, c, kv_all = attend((0, 1, 3), info, kvs, own, (qv1, qv3), (), False)
    o2, u, c, to_prev, to_next = attend((2,), info, (), (), (qv2,), (kv_all, u, c), True)
    from_next, from_prev = across_lines(to_prev, -1), across_lines(to_next, 1)

    v1, v3, v2 = along_line(o1, -1), along_line(o3, -3), along_line(o2, -2)
    base, base_other = project_near(place, (o0, v1, v3), v_own, v_other)
    m0, m1, m2, m3 = merge(me_arr, u, c, from_prev, from_next)
    given = project_far(place, v2, v_other, base_other, after=(m0,))
    video_out = project_far(place, v2, v_own, base, received=(swap(given),))

    a_mine = (m0, along_line(m3, 3), along_line(m2, 2), along_line(m1, 1))
    audio_out = project(place, a_mine, tuple(swap(m) for m in a_mine), a_own, a_other)
    return video_out, audio_out


def solution(mesh):
    in_specs = (
        P("seq", "head"),
        P("seq", "head"),
        P("seq", "head"),
        P("seq", "head"),
        P("head", None),
        P("head", None),
        P(),
        P(),
    )
    out_specs = (P("seq", "head"), P("seq", "head"))
    return jax.shard_map(shards, mesh=mesh, in_specs=in_specs, out_specs=out_specs, check_vma=False)
```

```python
import functools
import math

import jax
import jax.numpy as jnp
from jax import lax
from jax.experimental import pallas as pl
from jax.experimental.pallas import tpu as pltpu
from jax.sharding import PartitionSpec as P

HD = 128
LINE = 4
GH = 3
GW = GH * HD
VID = 512
AUD = 256
NEG = -1e30
SCALE = math.log2(math.e) / math.sqrt(HD)
EXTRA = 16
BF = jnp.bfloat16
F32 = jnp.float32
MIB = 2**20


def cost(us):
    return pl.CostEstimate(flops=int(us * 1e9), bytes_accessed=1000, transcendentals=0)


TINY = cost(0.001)
ANY = pl.BlockSpec(memory_space=pl.ANY)
SMEM = pl.BlockSpec(memory_space=pltpu.SMEM)
VMEM = pl.BlockSpec(memory_space=pltpu.VMEM)


def group_cols(g):
    return pl.ds(pl.multiple_of(g * GW, HD), GW)


def through(pieces, held, sem):
    ins = [pltpu.make_async_copy(src, held.at[at], sem.at[0, i]) for i, (src, at, _) in enumerate(pieces)]
    outs = [pltpu.make_async_copy(held.at[at], dst, sem.at[1, i]) for i, (_, at, dst) in enumerate(pieces)]
    for copy in ins:
        copy.start()
    for copy, out in zip(ins, outs):
        copy.wait()
        out.start()
    for copy in outs:
        copy.wait()


def pack_kernel(steps, me, a, b, *refs):
    outs, held, sem = refs[-len(steps) - 2 : -2], refs[-2], refs[-1]
    y = lax.rem(me[0], LINE)
    pieces = []
    for d, out in zip(steps, outs):
        cols = group_cols(lax.rem(y + d, LINE))
        pieces.append((a.at[:, cols], len(pieces), out.at[0]))
        pieces.append((b.at[:, cols], len(pieces), out.at[1]))
    through(pieces, held, sem)


def pack(steps, me, a, b, *after, limit=60):
    n = len(steps)
    return pl.pallas_call(
        functools.partial(pack_kernel, steps),
        out_shape=(jax.ShapeDtypeStruct((2, a.shape[0], GW), BF),) * n,
        in_specs=[SMEM] + [ANY] * (2 + len(after)),
        out_specs=(ANY,) * n,
        scratch_shapes=[pltpu.VMEM((2 * n, a.shape[0], GW), BF), pltpu.SemaphoreType.DMA((2, 2 * n))],
        compiler_params=pltpu.CompilerParams(vmem_limit_bytes=limit * MIB),
        cost_estimate=TINY,
        name="pack",
    )(me, a, b, *after)


def send_half_kernel(place, w, after, out, held, sem):
    width = out.shape[1]
    rows = held.shape[1]
    other = pl.ds(pl.multiple_of((1 - place[1]) * width, HD), width)
    through([(w.at[pl.ds(i * rows, rows), other], i, out.at[pl.ds(i * rows, rows)]) for i in range(4)], held, sem)


def half_to_send(place, w, after):
    rows, width = w.shape[0], w.shape[1] // 2
    return pl.pallas_call(
        send_half_kernel,
        out_shape=jax.ShapeDtypeStruct((rows, width), BF),
        in_specs=[SMEM, ANY, ANY],
        out_specs=ANY,
        scratch_shapes=[pltpu.VMEM((4, rows // 4, width), BF), pltpu.SemaphoreType.DMA((2, 4))],
        compiler_params=pltpu.CompilerParams(vmem_limit_bytes=60 * MIB),
        cost_estimate=cost(4),
        name="half_to_send",
    )(place, w, after)


def load_kernel(place, v, a, after, v_own, v_other, a_own, token, sem):
    width = v_own.shape[1]
    own = pl.ds(pl.multiple_of(place[1] * width, HD), width)
    other = pl.ds(pl.multiple_of((1 - place[1]) * width, HD), width)
    copies = [
        pltpu.make_async_copy(v.at[:, other], v_other, sem.at[0]),
        pltpu.make_async_copy(v.at[:, own], v_own, sem.at[1]),
        pltpu.make_async_copy(a.at[:, own], a_own, sem.at[2]),
    ]
    for copy in copies:
        copy.start()
    token[...] = jnp.zeros_like(token)
    for copy in copies:
        copy.wait()


def load_projections(place, v, a, after):
    rows, width = v.shape[0], v.shape[1] // 2
    half = jax.ShapeDtypeStruct((rows, width), BF)
    return pl.pallas_call(
        load_kernel,
        out_shape=(half,) * 3 + (jax.ShapeDtypeStruct((8, HD), F32),),
        in_specs=[SMEM, ANY, ANY, ANY],
        out_specs=(VMEM,) * 4,
        scratch_shapes=[pltpu.SemaphoreType.DMA((3,))],
        compiler_params=pltpu.CompilerParams(vmem_limit_bytes=44 * MIB),
        cost_estimate=cost(8),
        name="load_projections",
    )(place, v, a, after)


def line_kernel(me, k, v, kv1, kv2, kv3, after, low, high, held, sem):
    y = lax.rem(me[0], LINE)
    cols = group_cols(y)
    copies = [
        pltpu.make_async_copy(k.at[:, cols], held.at[y, 0], sem.at[0]),
        pltpu.make_async_copy(v.at[:, cols], held.at[y, 1], sem.at[4]),
    ]
    for d, got in ((1, kv1), (2, kv2), (3, kv3)):
        copies.append(pltpu.make_async_copy(got, held.at[lax.rem(y + LINE - d, LINE)], sem.at[d]))
    for copy in copies:
        copy.start()
    for copy in copies:
        copy.wait()
    copies = [
        pltpu.make_async_copy(held.at[pl.ds(0, 2)], low, sem.at[0]),
        pltpu.make_async_copy(held.at[pl.ds(2, 2)], high, sem.at[1]),
    ]
    for copy in copies:
        copy.start()
    for copy in copies:
        copy.wait()


def line_blocks(me, k, v, kv1, kv2, kv3, after):
    half = jax.ShapeDtypeStruct((2, 2, AUD, GW), BF)
    return pl.pallas_call(
        line_kernel,
        out_shape=(half, half),
        in_specs=[SMEM] + [ANY] * 6,
        out_specs=(ANY, ANY),
        scratch_shapes=[pltpu.VMEM((LINE, 2, AUD, GW), BF), pltpu.SemaphoreType.DMA((5,))],
        compiler_params=pltpu.CompilerParams(vmem_limit_bytes=16 * MIB),
        cost_estimate=TINY,
        name="line_blocks",
    )(me, k, v, kv1, kv2, kv3, after)


def attend_kernel(steps, own, carried, last, *refs):
    refs = list(refs)

    def take(n):
        part = refs[:n]
        del refs[:n]
        return part

    me, first, count = take(3)
    kvs = [] if carried else take(4)
    q_own, v_own, _, _ = take(4) if own else (None,) * 4
    arrived = take(len(steps) - (1 if own else 0))
    if carried:
        (kbuf,) = take(1)
        take(2)
    outs = take(len(steps))
    ubuf, csum = take(2)
    if not carried:
        (kbuf,) = take(1)
    if last:
        before, after = take(2)
    qbuf, tbuf, mbuf, cbuf, abuf, vtbuf, sem, qsem = refs

    y = lax.rem(me[0], LINE)
    base = me[0] - y
    copies = []

    def copy(src, dst):
        copies.append(pltpu.make_async_copy(src, dst, sem.at[len(copies)]))

    for i, part in enumerate(kvs):
        copy(part, kbuf.at[pl.ds(2 * i, 2)])
    if own:
        copy(q_own.at[:, group_cols(y)], qbuf.at[0, 0])
        copy(v_own.at[:, group_cols(y)], qbuf.at[0, 1])
    for c in copies:
        c.start()
    for i, part in enumerate(arrived):
        pltpu.make_async_copy(part, qbuf.at[i + (1 if own else 0)], qsem.at[i]).start()
    if not carried:
        csum[...] = jnp.full_like(csum, NEG)
    for c in copies:
        c.wait()

    diagonal = lax.broadcasted_iota(jnp.int32, (HD, HD), 0) == lax.broadcasted_iota(jnp.int32, (HD, HD), 1)
    unit = jnp.where(diagonal, 1.0, 0.0).astype(BF)

    def video(i, carry):
        if own:

            @pl.when(i > 0)
            def _():
                pltpu.make_async_copy(qbuf.at[i], qbuf.at[i], qsem.at[i - 1]).wait()

        else:
            pltpu.make_async_copy(qbuf.at[i], qbuf.at[i], qsem.at[i]).wait()
        step = jnp.int32(steps[0])
        for n in range(1, len(steps)):
            step = jnp.where(i == n, steps[n], step)
        v = lax.rem(y + LINE - step, LINE)
        lo = first[base + v] - base + 2
        hi = lo + count[base + v]
        def scores(a, carry):
            slot = a - lo
            for h in range(GH):
                cols = slice(h * HD, (h + 1) * HD)
                t = lax.dot_general(
                    qbuf[i, 0, :, cols], kbuf[a, 0, :, cols], (((1,), (1,)), ((), ())), preferred_element_type=F32
                )
                t = t * SCALE
                tbuf[h, slot] = t
                top = jnp.maximum(t[:, :HD], t[:, HD:])
                mbuf[h] = jnp.where(slot == 0, top, jnp.maximum(mbuf[h], top))
                cbuf[h, slot] = jnp.broadcast_to(jnp.max(t, axis=0, keepdims=True), (8, AUD))
            return carry

        lax.fori_loop(lo, hi, scores, 0)
        for h in range(GH):
            cols = slice(h * HD, (h + 1) * HD)
            mbuf[h] = jnp.broadcast_to(jnp.max(mbuf[h], axis=1, keepdims=True), (VID, HD))
            abuf[h] = jnp.zeros((VID, 2 * HD), F32)
            turned = lax.dot_general(
                unit, qbuf[i, 1, :, cols], (((1,), (1,)), ((), ())), preferred_element_type=F32
            )
            vtbuf[h, :HD] = turned.astype(BF)
            vtbuf[h, HD:] = jnp.ones((EXTRA, VID), BF)

        def weights(a, carry):
            slot = a - lo
            for h in range(GH):
                cols = slice(h * HD, (h + 1) * HD)
                t = tbuf[h, slot]
                r = mbuf[h]
                c = cbuf[h, slot, 0:1]
                by_row = jnp.exp2(t - jnp.concatenate([r, r], axis=1)).astype(BF)
                values = jnp.concatenate([kbuf[a, 1, :, cols], jnp.ones((AUD, HD), BF)], axis=1)
                abuf[h] += jnp.dot(by_row, values, preferred_element_type=F32)
                by_col = jnp.exp2(t - c).astype(BF)
                u = jnp.dot(vtbuf[h], by_col, preferred_element_type=F32)
                old = csum[h, a, 0:1]
                new = jnp.maximum(old, c)
                kept = jnp.where(old > NEG, ubuf[h, a], 0.0)
                ubuf[h, a] = kept * jnp.exp2(old - new) + u * jnp.exp2(c - new)
                csum[h, a] = jnp.broadcast_to(new, (8, AUD))
            return carry

        lax.fori_loop(lo, hi, weights, 0)
        for n, out in enumerate(outs):

            @pl.when(i == n)
            def _():
                for h in range(GH):
                    out[:, h * HD : (h + 1) * HD] = (abuf[h, :, :HD] / abuf[h, :, HD:]).astype(BF)

        return carry

    lax.fori_loop(0, len(steps), video, 0)

    if last:
        row = lax.broadcasted_iota(jnp.int32, (EXTRA, AUD), 0)
        for place, out in ((0, before), (6, after)):
            for j in range(2):
                levels = jnp.zeros((EXTRA, AUD), F32)
                for h in range(GH):
                    top = csum[h, place + j, 0:1]
                    some = top > NEG
                    n = jnp.where(some, ubuf[h, place + j, HD : HD + 1], 1.0)
                    u = jnp.where(some, ubuf[h, place + j, :HD], 0.0)
                    out[j, h * HD : (h + 1) * HD] = (u / n).astype(BF)
                    level = jnp.where(some, top + jnp.log2(n), NEG)
                    hi = level.astype(BF).astype(F32)
                    mid = (level - hi).astype(BF).astype(F32)
                    for k, part in enumerate((hi, mid, level - hi - mid)):
                        levels = jnp.where(row == 3 * h + k, part, levels)
                out[j, GW:] = levels.astype(BF)


def attend(steps, info, kvs, own, arrived, sums, last):
    n = len(steps)
    n_idx = 2 * LINE
    sum_shapes = [
        jax.ShapeDtypeStruct((GH, n_idx, HD + EXTRA, AUD), F32),
        jax.ShapeDtypeStruct((GH, n_idx, 8, AUD), F32),
    ]
    out_shape = [jax.ShapeDtypeStruct((VID, GW), BF)] * n + sum_shapes
    out_specs = [VMEM] * (n + 2)
    if last:
        out_shape += [jax.ShapeDtypeStruct((2, GW + EXTRA, AUD), BF)] * 2
        out_specs += [VMEM] * 2
    assert bool(own) != bool(sums)
    operands = [*info, *kvs, *own, *arrived, *sums]
    at = len(operands) - len(sums)
    if not sums:
        out_shape.append(jax.ShapeDtypeStruct((n_idx, 2, AUD, GW), BF))
        out_specs.append(VMEM)
    return pl.pallas_call(
        functools.partial(attend_kernel, steps, bool(own), bool(sums), last),
        out_shape=tuple(out_shape),
        in_specs=[SMEM] * 3 + [ANY] * (at - 3) + [VMEM] * len(sums),
        out_specs=tuple(out_specs),
        scratch_shapes=[
            pltpu.VMEM((n, 2, VID, GW), BF),
            pltpu.VMEM((GH, 5, VID, AUD), F32),
            pltpu.VMEM((GH, VID, HD), F32),
            pltpu.VMEM((GH, 5, 8, AUD), F32),
            pltpu.VMEM((GH, VID, 2 * HD), F32),
            pltpu.VMEM((GH, HD + EXTRA, VID), BF),
            pltpu.SemaphoreType.DMA((8,)),
            pltpu.SemaphoreType.DMA((2,)),
        ],
        input_output_aliases={at + 1: n, at + 2: n + 1} if sums else {},
        compiler_params=pltpu.CompilerParams(vmem_limit_bytes=18 * MIB),
        cost_estimate=cost(6 * n),
        name="attend_last" if last else "attend",
    )(*operands)


def merge_kernel(me, u, c, prev, nxt, out0, out1, out2, out3):
    y = lax.rem(me[0], LINE)
    for d, out in enumerate((out0, out1, out2, out3)):
        j = lax.rem(y + d, LINE)
        for h in range(GH):
            low = j < 2
            at = lax.rem(j, 2)
            rows = slice(h * HD, (h + 1) * HD)
            got = jnp.where(low, prev[at, rows].astype(F32), nxt[at, rows].astype(F32))
            levels = jnp.where(low, prev[at, GW:].astype(F32), nxt[at, GW:].astype(F32))
            level = levels[3 * h : 3 * h + 1] + levels[3 * h + 1 : 3 * h + 2] + levels[3 * h + 2 : 3 * h + 3]
            n = u[h, j + 2, HD : HD + 1]
            own = c[h, j + 2, 0:1] + jnp.log2(n)
            top = jnp.maximum(own, level)
            own_w = jnp.exp2(own - top)
            got_w = jnp.exp2(level - top)
            total = own_w + got_w
            mixed = u[h, j + 2, :HD] * (own_w / (n * total)) + got * (got_w / total)
            out[:, h * HD : (h + 1) * HD] = mixed.T.astype(BF)


def merge(me, u, c, prev, nxt):
    return pl.pallas_call(
        merge_kernel,
        out_shape=(jax.ShapeDtypeStruct((AUD, GW), BF),) * LINE,
        in_specs=[SMEM] + [VMEM] * 4,
        out_specs=(VMEM,) * LINE,
        name="merge",
        cost_estimate=TINY,
        compiler_params=pltpu.CompilerParams(vmem_limit_bytes=12 * MIB),
    )(me, u, c, prev, nxt)


def near_kernel(place, o0, o1, o3, w_own, w_other, own, other, held, sem):
    y = place[0]
    copies = [pltpu.make_async_copy(o, held.at[i], sem.at[i]) for i, o in enumerate((o0, o1, o3))]
    for copy in copies:
        copy.start()
    for copy in copies:
        copy.wait()
    for w, out in ((w_other, other), (w_own, own)):
        for i, d in enumerate((0, 1, 3)):
            rows = group_cols(lax.rem(y + d, LINE))
            part = jnp.dot(held[i], w[rows, :], preferred_element_type=F32)
            out[...] = part if i == 0 else out[...] + part


def project_near(place, near, w_own, w_other):
    rows, width = near[0].shape[0], w_own.shape[1]
    return pl.pallas_call(
        near_kernel,
        out_shape=(jax.ShapeDtypeStruct((rows, width), F32),) * 2,
        in_specs=[SMEM] + [ANY] * 3 + [VMEM] * 2,
        out_specs=(VMEM,) * 2,
        scratch_shapes=[pltpu.VMEM((3, rows, GW), BF), pltpu.SemaphoreType.DMA((3,))],
        compiler_params=pltpu.CompilerParams(vmem_limit_bytes=16 * MIB),
        cost_estimate=cost(4),
        name="project_near",
    )(place, *near, w_own, w_other)


def far_kernel(n_add, place, piece, w, *refs):
    adds = refs[:n_add]
    out, done, sem = refs[-3:]
    base, received = adds[0], adds[1:]
    tiles, _, tile = done.shape
    rows = group_cols(lax.rem(place[0] + 2, LINE))
    outs = []
    for n in range(tiles):
        cols = slice(n * tile, (n + 1) * tile)
        total = base[:, cols] + jnp.dot(piece[...], w[rows, cols], preferred_element_type=F32)
        if received:
            total += received[0][:, cols].astype(F32)
        if not received:
            out[:, cols] = total.astype(BF)
            continue
        done[n] = total.astype(BF)
        outs.append(pltpu.make_async_copy(done.at[n], out.at[:, pl.ds(n * tile, tile)], sem.at[n]))
        outs[-1].start()
    for copy in outs:
        copy.wait()


def project_far(place, piece, w, base, received=(), after=()):
    rows, width = piece.shape[0], w.shape[1]
    tile = 384
    return pl.pallas_call(
        functools.partial(far_kernel, 1 + len(received)),
        out_shape=jax.ShapeDtypeStruct((rows, width), BF),
        in_specs=[SMEM, VMEM, VMEM, VMEM] + [VMEM] * len(received) + [ANY] * len(after),
        out_specs=ANY if received else VMEM,
        scratch_shapes=[
            pltpu.VMEM((width // tile, rows, tile), BF),
            pltpu.SemaphoreType.DMA((8,)),
        ],
        compiler_params=pltpu.CompilerParams(vmem_limit_bytes=16 * MIB),
        cost_estimate=cost(0.5),
        name="project_far",
    )(place, piece, w, base, *received, *after)


def project_kernel(place, *refs):
    mine, theirs = refs[:LINE], refs[LINE : 2 * LINE]
    w_mine, w_theirs, out, left, right, held, sem = refs[2 * LINE :]
    y = place[0]
    tiles, _, tile = held.shape
    ins = []
    for d in range(LINE):
        cols = group_cols(lax.rem(y + d, LINE))
        ins.append(pltpu.make_async_copy(mine[d], left.at[:, cols], sem.at[0, d]))
        ins.append(pltpu.make_async_copy(theirs[d], right.at[:, cols], sem.at[1, d]))
    for copy in ins:
        copy.start()
    for copy in ins:
        copy.wait()
    outs = []
    for n in range(tiles):
        cols = slice(n * tile, (n + 1) * tile)
        total = jnp.dot(left[...], w_mine[:, cols], preferred_element_type=F32)
        total += jnp.dot(right[...], w_theirs[:, cols], preferred_element_type=F32)
        held[n] = total.astype(BF)
        outs.append(pltpu.make_async_copy(held.at[n], out.at[:, pl.ds(n * tile, tile)], sem.at[2, n]))
        outs[-1].start()
    for copy in outs:
        copy.wait()


def project(place, mine, theirs, w, w_theirs):
    rows, width = mine[0].shape[0], w.shape[1]
    tile = 256
    return pl.pallas_call(
        project_kernel,
        out_shape=jax.ShapeDtypeStruct((rows, width), BF),
        in_specs=[SMEM] + [ANY] * (2 * LINE) + [VMEM] * 2,
        out_specs=ANY,
        scratch_shapes=[
            pltpu.VMEM((rows, LINE * GW), BF),
            pltpu.VMEM((rows, LINE * GW), BF),
            pltpu.VMEM((width // tile, rows, tile), BF),
            pltpu.SemaphoreType.DMA((3, 8)),
        ],
        compiler_params=pltpu.CompilerParams(vmem_limit_bytes=16 * MIB),
        cost_estimate=cost(4),
        name="project",
    )(place, *mine, *theirs, w, w_theirs)


def shards(
    video_query, video_value, audio_key, audio_value, video_proj, audio_proj, pair_first, pair_count
):
    nblocks = lax.axis_size("seq")
    me = lax.axis_index("seq").astype(jnp.int32)
    core = lax.axis_index("head").astype(jnp.int32)
    me_arr = me[None]
    place = jnp.stack([lax.rem(me, LINE), core])

    def along_line(x, d):
        return lax.ppermute(
            x, "seq", [(s, s // LINE * LINE + (s + d) % LINE) for s in range(nblocks)]
        )

    def across_lines(x, d):
        return lax.ppermute(x, "seq", [(s, (s + d * LINE) % nblocks) for s in range(nblocks)])

    def swap(x):
        return lax.ppermute(x, "head", [(0, 1), (1, 0)])

    kv_out = pack((1, 2, 3), me_arr, audio_key, audio_value)
    kv = [along_line(piece, d + 1) for d, piece in enumerate(kv_out)]
    near1, near3 = pack((1, 3), me_arr, video_query, video_value, kv_out[0])
    qv1, qv3 = along_line(near1, 1), along_line(near3, 3)
    a_send = half_to_send(place, audio_proj, near1)
    a_other = swap(a_send)
    low, high = line_blocks(me_arr, audio_key, audio_value, *kv, a_send)
    before, after = across_lines(high, 1), across_lines(low, -1)
    v_own, v_other, a_own, token = load_projections(place, video_proj, audio_proj, low)
    (far,) = pack((2,), me_arr, video_query, video_value, low, limit=32)
    qv2 = along_line(far, 2)

    info = (me_arr, pair_first, pair_count)
    kvs = (before, low, high, after)
    own = (video_query, video_value, far, token)
    o0, o1, o3, u, c, kv_all = attend((0, 1, 3), info, kvs, own, (qv1, qv3), (), False)
    o2, u, c, to_prev, to_next = attend((2,), info, (), (), (qv2,), (kv_all, u, c), True)
    from_next, from_prev = across_lines(to_prev, -1), across_lines(to_next, 1)

    v1, v3, v2 = along_line(o1, -1), along_line(o3, -3), along_line(o2, -2)
    base, base_other = project_near(place, (o0, v1, v3), v_own, v_other)
    m0, m1, m2, m3 = merge(me_arr, u, c, from_prev, from_next)
    given = project_far(place, v2, v_other, base_other, after=(m0,))
    video_out = project_far(place, v2, v_own, base, received=(swap(given),))

    a_mine = (m0, along_line(m3, 3), along_line(m2, 2), along_line(m1, 1))
    audio_out = project(place, a_mine, tuple(swap(m) for m in a_mine), a_own, a_other)
    return video_out, audio_out


def solution(mesh):
    in_specs = (
        P("seq", "head"),
        P("seq", "head"),
        P("seq", "head"),
        P("seq", "head"),
        P("head", None),
        P("head", None),
        P(),
        P(),
    )
    out_specs = (P("seq", "head"), P("seq", "head"))
    return jax.shard_map(shards, mesh=mesh, in_specs=in_specs, out_specs=out_specs, check_vma=False)
```

```python
import functools
import math

import jax
import jax.numpy as jnp
from jax import lax
from jax.experimental import pallas as pl
from jax.experimental.pallas import tpu as pltpu
from jax.sharding import PartitionSpec as P

HD = 128
LINE = 4
GH = 3
GW = GH * HD
VID = 512
AUD = 256
NEG = -1e30
SCALE = math.log2(math.e) / math.sqrt(HD)
EXTRA = 16
BF = jnp.bfloat16
F32 = jnp.float32
MIB = 2**20


def cost(us):
    return pl.CostEstimate(flops=int(us * 1e9), bytes_accessed=1000, transcendentals=0)


TINY = cost(0.001)
ANY = pl.BlockSpec(memory_space=pl.ANY)
SMEM = pl.BlockSpec(memory_space=pltpu.SMEM)
VMEM = pl.BlockSpec(memory_space=pltpu.VMEM)


def group_cols(g):
    return pl.ds(pl.multiple_of(g * GW, HD), GW)


def through(pieces, held, sem):
    ins = [pltpu.make_async_copy(src, held.at[at], sem.at[0, i]) for i, (src, at, _) in enumerate(pieces)]
    outs = [pltpu.make_async_copy(held.at[at], dst, sem.at[1, i]) for i, (_, at, dst) in enumerate(pieces)]
    for copy in ins:
        copy.start()
    for copy, out in zip(ins, outs):
        copy.wait()
        out.start()
    for copy in outs:
        copy.wait()


def pack_kernel(steps, me, a, b, *refs):
    outs, held, sem = refs[-len(steps) - 2 : -2], refs[-2], refs[-1]
    y = lax.rem(me[0], LINE)
    pieces = []
    for d, out in zip(steps, outs):
        cols = group_cols(lax.rem(y + d, LINE))
        pieces.append((a.at[:, cols], len(pieces), out.at[0]))
        pieces.append((b.at[:, cols], len(pieces), out.at[1]))
    through(pieces, held, sem)


def pack(steps, me, a, b, *after, limit=60):
    n = len(steps)
    return pl.pallas_call(
        functools.partial(pack_kernel, steps),
        out_shape=(jax.ShapeDtypeStruct((2, a.shape[0], GW), BF),) * n,
        in_specs=[SMEM] + [ANY] * (2 + len(after)),
        out_specs=(ANY,) * n,
        scratch_shapes=[pltpu.VMEM((2 * n, a.shape[0], GW), BF), pltpu.SemaphoreType.DMA((2, 2 * n))],
        compiler_params=pltpu.CompilerParams(vmem_limit_bytes=limit * MIB),
        cost_estimate=TINY,
        name="pack",
    )(me, a, b, *after)


def send_half_kernel(place, w, after, out, held, sem):
    width = out.shape[1]
    rows = held.shape[1]
    other = pl.ds(pl.multiple_of((1 - place[1]) * width, HD), width)
    through([(w.at[pl.ds(i * rows, rows), other], i, out.at[pl.ds(i * rows, rows)]) for i in range(4)], held, sem)


def half_to_send(place, w, after):
    rows, width = w.shape[0], w.shape[1] // 2
    return pl.pallas_call(
        send_half_kernel,
        out_shape=jax.ShapeDtypeStruct((rows, width), BF),
        in_specs=[SMEM, ANY, ANY],
        out_specs=ANY,
        scratch_shapes=[pltpu.VMEM((4, rows // 4, width), BF), pltpu.SemaphoreType.DMA((2, 4))],
        compiler_params=pltpu.CompilerParams(vmem_limit_bytes=60 * MIB),
        cost_estimate=cost(4),
        name="half_to_send",
    )(place, w, after)


def load_kernel(place, v, a, after, v_own, v_other, a_own, token, sem):
    width = v_own.shape[1]
    own = pl.ds(pl.multiple_of(place[1] * width, HD), width)
    other = pl.ds(pl.multiple_of((1 - place[1]) * width, HD), width)
    copies = [
        pltpu.make_async_copy(v.at[:, other], v_other, sem.at[0]),
        pltpu.make_async_copy(v.at[:, own], v_own, sem.at[1]),
        pltpu.make_async_copy(a.at[:, own], a_own, sem.at[2]),
    ]
    for copy in copies:
        copy.start()
    token[...] = jnp.zeros_like(token)
    for copy in copies:
        copy.wait()


def load_projections(place, v, a, after):
    rows, width = v.shape[0], v.shape[1] // 2
    half = jax.ShapeDtypeStruct((rows, width), BF)
    return pl.pallas_call(
        load_kernel,
        out_shape=(half,) * 3 + (jax.ShapeDtypeStruct((8, HD), F32),),
        in_specs=[SMEM, ANY, ANY, ANY],
        out_specs=(VMEM,) * 4,
        scratch_shapes=[pltpu.SemaphoreType.DMA((3,))],
        compiler_params=pltpu.CompilerParams(vmem_limit_bytes=44 * MIB),
        cost_estimate=cost(8),
        name="load_projections",
    )(place, v, a, after)


def line_kernel(me, k, v, kv1, kv2, kv3, after, low, high, held, sem):
    y = lax.rem(me[0], LINE)
    cols = group_cols(y)
    copies = [
        pltpu.make_async_copy(k.at[:, cols], held.at[y, 0], sem.at[0]),
        pltpu.make_async_copy(v.at[:, cols], held.at[y, 1], sem.at[4]),
    ]
    for d, got in ((1, kv1), (2, kv2), (3, kv3)):
        copies.append(pltpu.make_async_copy(got, held.at[lax.rem(y + LINE - d, LINE)], sem.at[d]))
    for copy in copies:
        copy.start()
    for copy in copies:
        copy.wait()
    copies = [
        pltpu.make_async_copy(held.at[pl.ds(0, 2)], low, sem.at[0]),
        pltpu.make_async_copy(held.at[pl.ds(2, 2)], high, sem.at[1]),
    ]
    for copy in copies:
        copy.start()
    for copy in copies:
        copy.wait()


def line_blocks(me, k, v, kv1, kv2, kv3, after):
    half = jax.ShapeDtypeStruct((2, 2, AUD, GW), BF)
    return pl.pallas_call(
        line_kernel,
        out_shape=(half, half),
        in_specs=[SMEM] + [ANY] * 6,
        out_specs=(ANY, ANY),
        scratch_shapes=[pltpu.VMEM((LINE, 2, AUD, GW), BF), pltpu.SemaphoreType.DMA((5,))],
        compiler_params=pltpu.CompilerParams(vmem_limit_bytes=16 * MIB),
        cost_estimate=TINY,
        name="line_blocks",
    )(me, k, v, kv1, kv2, kv3, after)


def attend_kernel(steps, own, carried, last, *refs):
    refs = list(refs)

    def take(n):
        part = refs[:n]
        del refs[:n]
        return part

    me, first, count = take(3)
    kvs = [] if carried else take(4)
    q_own, v_own, _, _ = take(4) if own else (None,) * 4
    arrived = take(len(steps) - (1 if own else 0))
    if carried:
        (kbuf,) = take(1)
        take(2)
    outs = take(len(steps))
    ubuf, csum = take(2)
    if not carried:
        (kbuf,) = take(1)
    if last:
        before, after = take(2)
    qbuf, tbuf, mbuf, cbuf, abuf, vtbuf, sem, qsem = refs

    y = lax.rem(me[0], LINE)
    base = me[0] - y
    copies = []

    def copy(src, dst):
        copies.append(pltpu.make_async_copy(src, dst, sem.at[len(copies)]))

    for i, part in enumerate(kvs):
        copy(part, kbuf.at[pl.ds(2 * i, 2)])
    if own:
        copy(q_own.at[:, group_cols(y)], qbuf.at[0, 0])
        copy(v_own.at[:, group_cols(y)], qbuf.at[0, 1])
    for c in copies:
        c.start()
    for i, part in enumerate(arrived):
        pltpu.make_async_copy(part, qbuf.at[i + (1 if own else 0)], qsem.at[i]).start()
    if not carried:
        csum[...] = jnp.full_like(csum, NEG)
    for c in copies:
        c.wait()

    diagonal = lax.broadcasted_iota(jnp.int32, (HD, HD), 0) == lax.broadcasted_iota(jnp.int32, (HD, HD), 1)
    unit = jnp.where(diagonal, 1.0, 0.0).astype(BF)

    def video(i, carry):
        if own:

            @pl.when(i > 0)
            def _():
                pltpu.make_async_copy(qbuf.at[i], qbuf.at[i], qsem.at[i - 1]).wait()

        else:
            pltpu.make_async_copy(qbuf.at[i], qbuf.at[i], qsem.at[i]).wait()
        step = jnp.int32(steps[0])
        for n in range(1, len(steps)):
            step = jnp.where(i == n, steps[n], step)
        v = lax.rem(y + LINE - step, LINE)
        lo = first[base + v] - base + 2
        hi = lo + count[base + v]
        def scores(a, carry):
            slot = a - lo
            for h in range(GH):
                cols = slice(h * HD, (h + 1) * HD)
                t = lax.dot_general(
                    qbuf[i, 0, :, cols], kbuf[a, 0, :, cols], (((1,), (1,)), ((), ())), preferred_element_type=F32
                )
                t = t * SCALE
                tbuf[h, slot] = t
                top = jnp.maximum(t[:, :HD], t[:, HD:])
                mbuf[h] = jnp.where(slot == 0, top, jnp.maximum(mbuf[h], top))
                cbuf[h, slot] = jnp.broadcast_to(jnp.max(t, axis=0, keepdims=True), (8, AUD))
            return carry

        lax.fori_loop(lo, hi, scores, 0)
        for h in range(GH):
            cols = slice(h * HD, (h + 1) * HD)
            mbuf[h] = jnp.broadcast_to(jnp.max(mbuf[h], axis=1, keepdims=True), (VID, HD))
            abuf[h] = jnp.zeros((VID, 2 * HD), F32)
            turned = lax.dot_general(
                unit, qbuf[i, 1, :, cols], (((1,), (1,)), ((), ())), preferred_element_type=F32
            )
            vtbuf[h, :HD] = turned.astype(BF)
            vtbuf[h, HD:] = jnp.ones((EXTRA, VID), BF)

        def weights(a, carry):
            slot = a - lo
            for h in range(GH):
                cols = slice(h * HD, (h + 1) * HD)
                t = tbuf[h, slot]
                r = mbuf[h]
                c = cbuf[h, slot, 0:1]
                by_row = jnp.exp2(t - jnp.concatenate([r, r], axis=1)).astype(BF)
                values = jnp.concatenate([kbuf[a, 1, :, cols], jnp.ones((AUD, HD), BF)], axis=1)
                abuf[h] += jnp.dot(by_row, values, preferred_element_type=F32)
                by_col = jnp.exp2(t - c).astype(BF)
                u = jnp.dot(vtbuf[h], by_col, preferred_element_type=F32)
                old = csum[h, a, 0:1]
                new = jnp.maximum(old, c)
                kept = jnp.where(old > NEG, ubuf[h, a], 0.0)
                ubuf[h, a] = kept * jnp.exp2(old - new) + u * jnp.exp2(c - new)
                csum[h, a] = jnp.broadcast_to(new, (8, AUD))
            return carry

        lax.fori_loop(lo, hi, weights, 0)
        for n, out in enumerate(outs):

            @pl.when(i == n)
            def _():
                for h in range(GH):
                    out[:, h * HD : (h + 1) * HD] = (abuf[h, :, :HD] / abuf[h, :, HD:]).astype(BF)

        return carry

    lax.fori_loop(0, len(steps), video, 0)

    if last:
        row = lax.broadcasted_iota(jnp.int32, (EXTRA, AUD), 0)
        for place, out in ((0, before), (6, after)):
            for j in range(2):
                levels = jnp.zeros((EXTRA, AUD), F32)
                for h in range(GH):
                    top = csum[h, place + j, 0:1]
                    some = top > NEG
                    n = jnp.where(some, ubuf[h, place + j, HD : HD + 1], 1.0)
                    u = jnp.where(some, ubuf[h, place + j, :HD], 0.0)
                    out[j, h * HD : (h + 1) * HD] = (u / n).astype(BF)
                    level = jnp.where(some, top + jnp.log2(n), NEG)
                    hi = level.astype(BF).astype(F32)
                    mid = (level - hi).astype(BF).astype(F32)
                    for k, part in enumerate((hi, mid, level - hi - mid)):
                        levels = jnp.where(row == 3 * h + k, part, levels)
                out[j, GW:] = levels.astype(BF)


def attend(steps, info, kvs, own, arrived, sums, last):
    n = len(steps)
    n_idx = 2 * LINE
    sum_shapes = [
        jax.ShapeDtypeStruct((GH, n_idx, HD + EXTRA, AUD), F32),
        jax.ShapeDtypeStruct((GH, n_idx, 8, AUD), F32),
    ]
    out_shape = [jax.ShapeDtypeStruct((VID, GW), BF)] * n + sum_shapes
    out_specs = [VMEM] * (n + 2)
    if last:
        out_shape += [jax.ShapeDtypeStruct((2, GW + EXTRA, AUD), BF)] * 2
        out_specs += [VMEM] * 2
    assert bool(own) != bool(sums)
    operands = [*info, *kvs, *own, *arrived, *sums]
    at = len(operands) - len(sums)
    if not sums:
        out_shape.append(jax.ShapeDtypeStruct((n_idx, 2, AUD, GW), BF))
        out_specs.append(VMEM)
    return pl.pallas_call(
        functools.partial(attend_kernel, steps, bool(own), bool(sums), last),
        out_shape=tuple(out_shape),
        in_specs=[SMEM] * 3 + [ANY] * (at - 3) + [VMEM] * len(sums),
        out_specs=tuple(out_specs),
        scratch_shapes=[
            pltpu.VMEM((n, 2, VID, GW), BF),
            pltpu.VMEM((GH, 5, VID, AUD), F32),
            pltpu.VMEM((GH, VID, HD), F32),
            pltpu.VMEM((GH, 5, 8, AUD), F32),
            pltpu.VMEM((GH, VID, 2 * HD), F32),
            pltpu.VMEM((GH, HD + EXTRA, VID), BF),
            pltpu.SemaphoreType.DMA((8,)),
            pltpu.SemaphoreType.DMA((2,)),
        ],
        input_output_aliases={at + 1: n, at + 2: n + 1} if sums else {},
        compiler_params=pltpu.CompilerParams(vmem_limit_bytes=18 * MIB),
        cost_estimate=cost(6 * n),
        name="attend_last" if last else "attend",
    )(*operands)


def merge_kernel(me, u, c, prev, nxt, out0, out1, out2, out3):
    y = lax.rem(me[0], LINE)
    for d, out in enumerate((out0, out1, out2, out3)):
        j = lax.rem(y + d, LINE)
        for h in range(GH):
            low = j < 2
            at = lax.rem(j, 2)
            rows = slice(h * HD, (h + 1) * HD)
            got = jnp.where(low, prev[at, rows].astype(F32), nxt[at, rows].astype(F32))
            levels = jnp.where(low, prev[at, GW:].astype(F32), nxt[at, GW:].astype(F32))
            level = levels[3 * h : 3 * h + 1] + levels[3 * h + 1 : 3 * h + 2] + levels[3 * h + 2 : 3 * h + 3]
            n = u[h, j + 2, HD : HD + 1]
            own = c[h, j + 2, 0:1] + jnp.log2(n)
            top = jnp.maximum(own, level)
            own_w = jnp.exp2(own - top)
            got_w = jnp.exp2(level - top)
            total = own_w + got_w
            mixed = u[h, j + 2, :HD] * (own_w / (n * total)) + got * (got_w / total)
            out[:, h * HD : (h + 1) * HD] = mixed.T.astype(BF)


def merge(me, u, c, prev, nxt):
    return pl.pallas_call(
        merge_kernel,
        out_shape=(jax.ShapeDtypeStruct((AUD, GW), BF),) * LINE,
        in_specs=[SMEM] + [VMEM] * 4,
        out_specs=(VMEM,) * LINE,
        name="merge",
        cost_estimate=TINY,
        compiler_params=pltpu.CompilerParams(vmem_limit_bytes=12 * MIB),
    )(me, u, c, prev, nxt)


def near_kernel(place, o0, o1, o3, w_own, w_other, own, other, held, sem):
    y = place[0]
    copies = [pltpu.make_async_copy(o, held.at[i], sem.at[i]) for i, o in enumerate((o0, o1, o3))]
    for copy in copies:
        copy.start()
    for copy in copies:
        copy.wait()
    for w, out in ((w_other, other), (w_own, own)):
        for i, d in enumerate((0, 1, 3)):
            rows = group_cols(lax.rem(y + d, LINE))
            part = jnp.dot(held[i], w[rows, :], preferred_element_type=F32)
            out[...] = part if i == 0 else out[...] + part


def project_near(place, near, w_own, w_other):
    rows, width = near[0].shape[0], w_own.shape[1]
    return pl.pallas_call(
        near_kernel,
        out_shape=(jax.ShapeDtypeStruct((rows, width), F32),) * 2,
        in_specs=[SMEM] + [ANY] * 3 + [VMEM] * 2,
        out_specs=(VMEM,) * 2,
        scratch_shapes=[pltpu.VMEM((3, rows, GW), BF), pltpu.SemaphoreType.DMA((3,))],
        compiler_params=pltpu.CompilerParams(vmem_limit_bytes=16 * MIB),
        cost_estimate=cost(4),
        name="project_near",
    )(place, *near, w_own, w_other)


def far_kernel(n_add, place, piece, w, *refs):
    adds = refs[:n_add]
    out, done, sem = refs[-3:]
    base, received = adds[0], adds[1:]
    tiles, _, tile = done.shape
    rows = group_cols(lax.rem(place[0] + 2, LINE))
    outs = []
    for n in range(tiles):
        cols = slice(n * tile, (n + 1) * tile)
        total = base[:, cols] + jnp.dot(piece[...], w[rows, cols], preferred_element_type=F32)
        if received:
            total += received[0][:, cols].astype(F32)
        if not received:
            out[:, cols] = total.astype(BF)
            continue
        done[n] = total.astype(BF)
        outs.append(pltpu.make_async_copy(done.at[n], out.at[:, pl.ds(n * tile, tile)], sem.at[n]))
        outs[-1].start()
    for copy in outs:
        copy.wait()


def project_far(place, piece, w, base, received=(), after=()):
    rows, width = piece.shape[0], w.shape[1]
    tile = 512
    return pl.pallas_call(
        functools.partial(far_kernel, 1 + len(received)),
        out_shape=jax.ShapeDtypeStruct((rows, width), BF),
        in_specs=[SMEM, VMEM, VMEM, VMEM] + [VMEM] * len(received) + [ANY] * len(after),
        out_specs=ANY if received else VMEM,
        scratch_shapes=[
            pltpu.VMEM((width // tile, rows, tile), BF),
            pltpu.SemaphoreType.DMA((8,)),
        ],
        compiler_params=pltpu.CompilerParams(vmem_limit_bytes=16 * MIB),
        cost_estimate=cost(0.5),
        name="project_far",
    )(place, piece, w, base, *received, *after)


def project_kernel(place, *refs):
    mine, theirs = refs[:LINE], refs[LINE : 2 * LINE]
    w_mine, w_theirs, out, left, right, held, sem = refs[2 * LINE :]
    y = place[0]
    tiles, _, tile = held.shape
    ins = []
    for d in range(LINE):
        cols = group_cols(lax.rem(y + d, LINE))
        ins.append(pltpu.make_async_copy(mine[d], left.at[:, cols], sem.at[0, d]))
        ins.append(pltpu.make_async_copy(theirs[d], right.at[:, cols], sem.at[1, d]))
    for copy in ins:
        copy.start()
    for copy in ins:
        copy.wait()
    outs = []
    for n in range(tiles):
        cols = slice(n * tile, (n + 1) * tile)
        total = jnp.dot(left[...], w_mine[:, cols], preferred_element_type=F32)
        total += jnp.dot(right[...], w_theirs[:, cols], preferred_element_type=F32)
        held[n] = total.astype(BF)
        outs.append(pltpu.make_async_copy(held.at[n], out.at[:, pl.ds(n * tile, tile)], sem.at[2, n]))
        outs[-1].start()
    for copy in outs:
        copy.wait()


def project(place, mine, theirs, w, w_theirs):
    rows, width = mine[0].shape[0], w.shape[1]
    tile = 512
    return pl.pallas_call(
        project_kernel,
        out_shape=jax.ShapeDtypeStruct((rows, width), BF),
        in_specs=[SMEM] + [ANY] * (2 * LINE) + [VMEM] * 2,
        out_specs=ANY,
        scratch_shapes=[
            pltpu.VMEM((rows, LINE * GW), BF),
            pltpu.VMEM((rows, LINE * GW), BF),
            pltpu.VMEM((width // tile, rows, tile), BF),
            pltpu.SemaphoreType.DMA((3, 8)),
        ],
        compiler_params=pltpu.CompilerParams(vmem_limit_bytes=16 * MIB),
        cost_estimate=cost(4),
        name="project",
    )(place, *mine, *theirs, w, w_theirs)


def shards(
    video_query, video_value, audio_key, audio_value, video_proj, audio_proj, pair_first, pair_count
):
    nblocks = lax.axis_size("seq")
    me = lax.axis_index("seq").astype(jnp.int32)
    core = lax.axis_index("head").astype(jnp.int32)
    me_arr = me[None]
    place = jnp.stack([lax.rem(me, LINE), core])

    def along_line(x, d):
        return lax.ppermute(
            x, "seq", [(s, s // LINE * LINE + (s + d) % LINE) for s in range(nblocks)]
        )

    def across_lines(x, d):
        return lax.ppermute(x, "seq", [(s, (s + d * LINE) % nblocks) for s in range(nblocks)])

    def swap(x):
        return lax.ppermute(x, "head", [(0, 1), (1, 0)])

    kv_out = pack((1, 2, 3), me_arr, audio_key, audio_value)
    kv = [along_line(piece, d + 1) for d, piece in enumerate(kv_out)]
    near1, near3 = pack((1, 3), me_arr, video_query, video_value, kv_out[0])
    qv1, qv3 = along_line(near1, 1), along_line(near3, 3)
    a_send = half_to_send(place, audio_proj, near1)
    a_other = swap(a_send)
    low, high = line_blocks(me_arr, audio_key, audio_value, *kv, a_send)
    before, after = across_lines(high, 1), across_lines(low, -1)
    v_own, v_other, a_own, token = load_projections(place, video_proj, audio_proj, low)
    (far,) = pack((2,), me_arr, video_query, video_value, low, limit=32)
    qv2 = along_line(far, 2)

    info = (me_arr, pair_first, pair_count)
    kvs = (before, low, high, after)
    own = (video_query, video_value, far, token)
    o0, o1, o3, u, c, kv_all = attend((0, 1, 3), info, kvs, own, (qv1, qv3), (), False)
    o2, u, c, to_prev, to_next = attend((2,), info, (), (), (qv2,), (kv_all, u, c), True)
    from_next, from_prev = across_lines(to_prev, -1), across_lines(to_next, 1)

    v1, v3, v2 = along_line(o1, -1), along_line(o3, -3), along_line(o2, -2)
    base, base_other = project_near(place, (o0, v1, v3), v_own, v_other)
    m0, m1, m2, m3 = merge(me_arr, u, c, from_prev, from_next)
    given = project_far(place, v2, v_other, base_other, after=(m0,))
    video_out = project_far(place, v2, v_own, base, received=(swap(given),))

    a_mine = (m0, along_line(m3, 3), along_line(m2, 2), along_line(m1, 1))
    audio_out = project(place, a_mine, tuple(swap(m) for m in a_mine), a_own, a_other)
    return video_out, audio_out


def solution(mesh):
    in_specs = (
        P("seq", "head"),
        P("seq", "head"),
        P("seq", "head"),
        P("seq", "head"),
        P("head", None),
        P("head", None),
        P(),
        P(),
    )
    out_specs = (P("seq", "head"), P("seq", "head"))
    return jax.shard_map(shards, mesh=mesh, in_specs=in_specs, out_specs=out_specs, check_vma=False)
```
